128 devices in a mesh: dp: 16 (over z_lo, y, core), seq: 8 (over x, z_hi).
Axes of the slice: x: 4, y: 4, z: 4 (z_hi: 2, z_lo: 2; z = z_hi * 2 + z_lo), core: 2. Of those that a mesh axis runs over, the one named last changes fastest.
Arguments:
- tokens: bfloat16 [16, 16, 256, 1152], P('dp', 'seq'), may hold values from -6 to 6
- mod_shift: float32 [16, 1152], P('dp'), may hold values from -3 to 3
- mod_scale: float32 [16, 1152], P('dp'), may hold values from -2.5 to 2.5
- res_gate: float32 [16, 1152], P('dp'), may hold values from -4 to 4
- qkv_weight: bfloat16 [1152, 3456], replicated, may hold values from -0.1875 to 0.1875
- out_weight: bfloat16 [1152, 1152], replicated, may hold values from -0.1875 to 0.1875
- query_gain: float32 [72], replicated, may hold values from 0.1 to 1.9
- key_gain: float32 [72], replicated, may hold values from 0.1 to 1.9
- cotangent: bfloat16 [16, 16, 256, 1152], P('dp', 'seq'), may hold values from -6 to 6
Outputs:
- block_output: bfloat16 [16, 16, 256, 1152], P('dp', 'seq')
- grad_tokens: bfloat16 [16, 16, 256, 1152], P('dp', 'seq')
- grad_qkv_weight: bfloat16 [1152, 3456], P(('dp', 'seq'))
- grad_out_weight: bfloat16 [1152, 1152], P(('dp', 'seq'))
The draws below stay inside these ranges and needn't reach their ends.
All inputs are finite; a program needn't handle non-finite values.
Results may differ from the reference program's by a relative error of at most 0.019.
Values may be sent and summed in bfloat16 or wider, within the bound.
A program may use at most 192 MiB of HBM per device.

```python
import jax
import jax.numpy as jnp
from jax import lax

D = 1152
HEAD_DIM = 72
FRAMES = 16
POS = 256
VIDEOS = 16


def level_of(own_key, dims, shards, least, top_value):
    factor_of = 1.0
    for dim, parts in shards:
        draws = jax.random.uniform(jax.random.fold_in(jax.random.fold_in(own_key, 6), dim), (parts,), jnp.float32, least / len(shards), top_value / len(shards))
        factor_of = factor_of * jnp.repeat(jnp.exp(draws), dims[dim] // parts).reshape((-1,) + (1,) * (len(dims) - 1 - dim))
    return factor_of


def normal_values(rng, dims, scale, bound, pieces=(), dtype=jnp.bfloat16):
    values = jax.random.normal(rng, dims, jnp.float32) * scale
    if len(pieces) > 0:
        values = level_of(rng, dims, pieces, -0.22, 0.18) * values
    return jnp.clip(values, min=-bound, max=bound).astype(dtype)


def setup_inputs(seed: int = 0) -> dict:
    key_of = jax.random.split(jax.random.key(seed), 10)
    tokens = normal_values(key_of[0], (VIDEOS, FRAMES, POS, D), 1.0, 6.0, ((0, 16), (1, 8)))
    mod_shift = normal_values(key_of[1], (VIDEOS, D), 0.5, 3.0, ((0, 16),), jnp.float32)
    mod_scale = normal_values(key_of[2], (VIDEOS, D), 0.5, 2.5, ((0, 16),), jnp.float32)
    res_gate = normal_values(key_of[3], (VIDEOS, D), 1.0, 4.0, ((0, 16),), jnp.float32)
    qkv_weight = normal_values(key_of[4], (D, 3 * D), D ** -0.5, 0.1875)
    out_weight = normal_values(key_of[5], (D, D), D ** -0.5, 0.1875)
    query_gain = jnp.clip(1.0 + 0.18 * jax.random.normal(key_of[6], (HEAD_DIM,), jnp.float32), 0.1, 1.9)
    key_gain = jnp.clip(1.0 + 0.18 * jax.random.normal(key_of[7], (HEAD_DIM,), jnp.float32), 0.1, 1.9)
    cotangent = normal_values(key_of[8], (VIDEOS, FRAMES, POS, D), 1.0, 6.0, ((0, 16), (1, 8)))
    return {"tokens": tokens, "mod_shift": mod_shift, "mod_scale": mod_scale, "res_gate": res_gate, "qkv_weight": qkv_weight, "out_weight": out_weight, "query_gain": query_gain, "key_gain": key_gain, "cotangent": cotangent}


def modulate(tokens_f32, mod_shift, mod_scale):
    row_mean = lax.optimization_barrier(jnp.mean(tokens_f32, axis=-1, keepdims=True))
    centered = tokens_f32 - row_mean
    variance = lax.optimization_barrier(jnp.mean(centered * centered, axis=-1, keepdims=True))
    normed = centered * lax.rsqrt(variance + 1e-06)
    return normed * (1.0 + mod_scale[:, None, None, :]) + mod_shift[:, None, None, :]

def rms_gain(inputs, gain_vector, factor):
    as_float = inputs.astype(jnp.float32)
    mean_square = lax.optimization_barrier(jnp.mean(as_float * as_float, axis=-1, keepdims=True))
    return (as_float * lax.rsqrt(mean_square + 1e-06) * gain_vector * factor).astype(jnp.bfloat16)

def attend(queries, key_block, value_block, query_gain, key_gain):
    head_dim = query_gain.shape[0]
    num_heads = queries.shape[-1] // head_dim

    def split_heads(tensor):
        return tensor.reshape(tensor.shape[:3] + (num_heads, head_dim))
    query_norm = rms_gain(split_heads(queries), query_gain, head_dim ** (-0.5))
    key_norm = rms_gain(split_heads(key_block), key_gain, 1.0)
    scores = jnp.einsum('vfphd,vgphd->vphfg', query_norm, key_norm, preferred_element_type=jnp.float32)
    weights = jnp.exp(scores)
    probabilities = (weights / lax.optimization_barrier(jnp.sum(weights, axis=-1, keepdims=True))).astype(jnp.bfloat16)
    result = jnp.einsum('vphfg,vgphd->vfphd', probabilities, split_heads(value_block), preferred_element_type=jnp.float32)
    return result.reshape(queries.shape).astype(jnp.bfloat16)

def flat_dot(left_side, right_side):
    flattened = left_side.reshape(-1, left_side.shape[-1])
    product = jnp.dot(flattened, right_side, preferred_element_type=jnp.float32)
    return product.reshape(left_side.shape[:-1] + (right_side.shape[-1],))

def flat_dot_t(left_side, right_side):
    flattened = left_side.reshape(-1, left_side.shape[-1])
    product = lax.dot_general(flattened, right_side, (((1,), (1,)), ((), ())), preferred_element_type=jnp.float32)
    return product.reshape(left_side.shape[:-1] + (right_side.shape[0],))

def token_outer(left_side, right_side):
    left_rows = left_side.reshape(-1, left_side.shape[-1])
    right_rows = right_side.reshape(-1, right_side.shape[-1])
    return lax.dot_general(left_rows, right_rows, (((0,), (0,)), ((), ())), preferred_element_type=jnp.float32)

def reference(tokens, mod_shift, mod_scale, res_gate, qkv_weight, out_weight, query_gain, key_gain, cotangent):
    width = tokens.shape[-1]
    tokens_f32 = tokens.astype(jnp.float32)
    modulated, pull_mod = jax.vjp(lambda tensor: modulate(tensor, mod_shift, mod_scale), tokens_f32)
    hidden = modulated.astype(jnp.bfloat16)
    projected = flat_dot(hidden, qkv_weight).astype(jnp.bfloat16)
    queries = projected[..., :width]
    key_block = projected[..., width:2 * width]
    value_block = projected[..., 2 * width:]
    attended, pull_att = jax.vjp(lambda first, second, third: attend(first, second, third, query_gain, key_gain), queries, key_block, value_block)
    projection = flat_dot(attended, out_weight)
    gate_bcast = res_gate[:, None, None, :]
    block_output = (tokens_f32 + gate_bcast * projection).astype(jnp.bfloat16)
    grad_projection = (cotangent.astype(jnp.float32) * gate_bcast).astype(jnp.bfloat16)
    grad_out_weight = token_outer(attended, grad_projection)
    grad_attended = flat_dot_t(grad_projection, out_weight).astype(jnp.bfloat16)
    grad_query, grad_keys, grad_values = pull_att(grad_attended)
    grad_projected = jnp.concatenate([grad_query, grad_keys, grad_values], axis=-1)
    grad_qkv_weight = token_outer(hidden, grad_projected)
    grad_hidden = flat_dot_t(grad_projected, qkv_weight).astype(jnp.bfloat16)
    grad_mod, = pull_mod(grad_hidden.astype(jnp.float32))
    grad_tokens = (cotangent.astype(jnp.float32) + grad_mod).astype(jnp.bfloat16)
    return (block_output, grad_tokens, grad_qkv_weight.astype(jnp.bfloat16), grad_out_weight.astype(jnp.bfloat16))
```

```python
import jax
import jax.numpy as jnp
from jax import lax
from jax.experimental import pallas as pl
from jax.experimental.pallas import tpu as pltpu
from jax.sharding import PartitionSpec as P

F32 = jnp.float32
BF16 = jnp.bfloat16
D = 1152
HD = 72
NH = 16


def dot_nn(a, b):
    return lax.dot_general(a, b, (((1,), (0,)), ((), ())), preferred_element_type=F32)


def dot_nt(a, b):
    return lax.dot_general(a, b, (((1,), (1,)), ((), ())), preferred_element_type=F32)


def dot_tn(a, b):
    return lax.dot_general(a, b, (((0,), (0,)), ((), ())), preferred_element_type=F32)


def ln_stats(x):
    mean = jnp.mean(x, axis=-1, keepdims=True)
    xc = x - mean
    var = jnp.mean(xc * xc, axis=-1, keepdims=True)
    return xc, lax.rsqrt(var + 1e-6)


CH = 32


def compute_kernel(tok, cot, shift, scale, gate, wqkv, wo, qg, kg, out, gtok, gw,
                   hid, proj, gp, gatt, att, dproj, hidt):
    n = tok.shape[0]
    groups = n // 256

    def phase_a(i, c):
        r = pl.ds(pl.multiple_of(i * CH, CH), CH)
        x = tok[r, :].astype(F32)
        xc, rs = ln_stats(x)
        hid[r, :] = (xc * rs * (1.0 + scale[...]) + shift[...]).astype(BF16)
        gp[r, :] = (cot[r, :].astype(F32) * gate[...]).astype(BF16)
        return c

    lax.fori_loop(0, n // CH, phase_a, 0)
    for b in range(3):
        cs = pl.ds(b * D, D)
        proj[:, cs] = dot_nn(hid[...], wqkv[:, cs]).astype(BF16)
    gatt[...] = dot_nt(gp[...], wo[...]).astype(BF16)

    ri = lax.broadcasted_iota(jnp.int32, (256, 256), 0)
    ci = lax.broadcasted_iota(jnp.int32, (256, 256), 1)
    mask = jnp.where((ri & 15) == (ci & 15), 1.0, 0.0).astype(F32)
    qgain = qg[...] * (HD ** -0.5)
    kgain = kg[...]

    def phase_c(g, c):
        r = pl.ds(pl.multiple_of(g * 256, 256), 256)
        for h in range(NH):
            q = proj[r, pl.ds(h * HD, HD)].astype(F32)
            k = proj[r, pl.ds(D + h * HD, HD)].astype(F32)
            v = proj[r, pl.ds(2 * D + h * HD, HD)]
            da = gatt[r, pl.ds(h * HD, HD)]
            rq = lax.rsqrt(jnp.mean(q * q, axis=-1, keepdims=True) + 1e-6)
            rk = lax.rsqrt(jnp.mean(k * k, axis=-1, keepdims=True) + 1e-6)
            qh = q * rq
            kh = k * rk
            qn = (qh * qgain).astype(BF16)
            kn = (kh * kgain).astype(BF16)
            s = dot_nt(qn, kn)
            e = jnp.exp(s) * mask
            p = e * (1.0 / jnp.sum(e, axis=-1, keepdims=True))
            pb = p.astype(BF16)
            a = dot_nn(pb, v)
            ab = a.astype(BF16)
            att[r, pl.ds(h * HD, HD)] = ab
            dp = dot_nt(da, v)
            delta = jnp.sum(da.astype(F32) * a, axis=-1, keepdims=True)
            ds = (p * (dp - delta)).astype(BF16)
            dv = dot_tn(pb, da)
            dqn = dot_nn(ds, kn) * qgain
            dkn = dot_tn(ds, qn) * kgain
            dq = rq * (dqn - qh * jnp.mean(dqn * qh, axis=-1, keepdims=True))
            dk = rk * (dkn - kh * jnp.mean(dkn * kh, axis=-1, keepdims=True))
            dproj[r, pl.ds(h * HD, HD)] = dq.astype(BF16)
            dproj[r, pl.ds(D + h * HD, HD)] = dk.astype(BF16)
            dproj[r, pl.ds(2 * D + h * HD, HD)] = dv.astype(BF16)
        return c

    lax.fori_loop(0, groups, phase_c, 0)

    po = dot_nn(att[...], wo[...])
    out[...] = (tok[...].astype(F32) + gate[...] * po).astype(BF16)

    hidt[...] = att[...].T
    gw[:, 3 * D:] = dot_nn(hidt[...], gp[...]).astype(BF16)
    hidt[...] = hid[...].T
    for b in range(3):
        cs = pl.ds(b * D, D)
        gw[:, cs] = dot_nn(hidt[...], dproj[:, cs]).astype(BF16)

    gp[...] = dot_nt(dproj[...], wqkv[...]).astype(BF16)

    def phase_f(i, c):
        r = pl.ds(pl.multiple_of(i * CH, CH), CH)
        x = tok[r, :].astype(F32)
        xc, rs = ln_stats(x)
        xh = xc * rs
        gm = gp[r, :].astype(F32) * (1.0 + scale[...])
        gx = rs * (gm - jnp.mean(gm, axis=-1, keepdims=True)
                   - xh * jnp.mean(gm * xh, axis=-1, keepdims=True))
        gtok[r, :] = (cot[r, :].astype(F32) + gx).astype(BF16)
        return c

    lax.fori_loop(0, n // CH, phase_f, 0)


def compute(tok, cot, shift, scale, gate, wqkv, wo, qg, kg):
    n = tok.shape[0]
    vm = pl.BlockSpec(memory_space=pltpu.VMEM)
    return pl.pallas_call(
        compute_kernel,
        out_shape=(
            jax.ShapeDtypeStruct((n, D), BF16),
            jax.ShapeDtypeStruct((n, D), BF16),
            jax.ShapeDtypeStruct((D, 4 * D), BF16),
        ),
        in_specs=[vm] * 9,
        out_specs=(vm,) * 3,
        scratch_shapes=[
            pltpu.VMEM((n, D), BF16),
            pltpu.VMEM((n, 3 * D), BF16),
            pltpu.VMEM((n, D), BF16),
            pltpu.VMEM((n, D), BF16),
            pltpu.VMEM((n, D), BF16),
            pltpu.VMEM((n, 3 * D), BF16),
            pltpu.VMEM((D, n), BF16),
        ],
        compiler_params=pltpu.CompilerParams(vmem_limit_bytes=56 * 1024 * 1024),
        cost_estimate=pl.CostEstimate(flops=2 * n * D * 12 * D, bytes_accessed=30 * 2**20, transcendentals=0),
    )(tok, cot, shift, scale, gate, wqkv, wo, qg, kg)


def to_groups(x):
    y = lax.all_to_all(x[0], "seq", split_axis=1, concat_axis=0, tiled=True)
    f, p, d = y.shape
    return y.reshape(f, p // 16, 16, d).transpose(1, 0, 2, 3).reshape(f * p, d)


def from_groups(y, frames, pos):
    z = y.reshape(pos // 16, frames, 16, D).transpose(1, 0, 2, 3).reshape(frames, pos, D)
    return lax.all_to_all(z, "seq", split_axis=0, concat_axis=1, tiled=True)[None]


def on_device(tokens, mod_shift, mod_scale, res_gate, qkv_weight, out_weight, query_gain, key_gain, cotangent):
    tok = to_groups(tokens)
    cot = to_groups(cotangent)
    n = tok.shape[0]
    out, gtok, gw = compute(tok, cot, mod_shift, mod_scale, res_gate, qkv_weight, out_weight,
                            query_gain[None], key_gain[None])
    block_output = from_groups(out, 16, n // 16)
    grad_tokens = from_groups(gtok, 16, n // 16)
    summed = lax.psum_scatter(gw, ("dp", "seq"), scatter_dimension=0, tiled=True)
    return block_output, grad_tokens, summed[:, : 3 * D], summed[:, 3 * D :]


def solution(mesh):
    tok = P("dp", "seq", None, None)
    vec = P("dp", None)
    return jax.shard_map(
        on_device,
        mesh=mesh,
        in_specs=(tok, vec, vec, vec, P(), P(), P(), P(), tok),
        out_specs=(tok, tok, P(("dp", "seq"), None), P(("dp", "seq"), None)),
        check_vma=False,
    )
```

```python
import numpy as np
import jax
import jax.numpy as jnp
from jax import lax
from jax.experimental import pallas as pl
from jax.experimental.pallas import tpu as pltpu
from jax.sharding import PartitionSpec as P

F32 = jnp.float32
BF16 = jnp.bfloat16
D = 1152
MESH = pl.DeviceIdType.MESH
PARTS = 4
ORDERS = ((1, 0, 2), (0, 2, 1), (2, 1, 0), (1, 2, 0))
RA, RB = 80, 64


def natural_rows():
    i = np.arange(D)
    core, rest = i // 576, i % 576
    a = (rest // 144, (rest // 36) % 4, (rest // 9) % 4)
    j = rest % 9
    table = np.zeros((D, PARTS), np.int32)
    for p, order in enumerate(ORDERS):
        c = [None] * 3
        for place, dim in enumerate(order):
            c[dim] = a[place]
        x, y, z = c
        table[:, p] = 9 * ((z % 2) * 64 + y * 16 + core * 8 + x * 2 + z // 2) + j
    return table


def spread(rows_from, rows_to):
    m = np.zeros((4 * rows_to, 4 * rows_from), np.float32)
    for b in range(4):
        for j in range(rows_from):
            m[b * rows_to + j, b * rows_from + j] = 1.0
    return m


def coords():
    dp = lax.axis_index("dp")
    sq = lax.axis_index("seq")
    z = lax.rem(sq, 2) * 2 + dp // 8
    return (sq // 2, lax.rem(dp // 2, 4), z), lax.rem(dp, 2)


def device(xyz, core):
    x, y, z = xyz
    return (lax.rem(z, 2) * 8 + y * 2 + core, x * 2 + z // 2)


def shifted(xyz, dim, k):
    out = list(xyz)
    out[dim] = lax.rem(xyz[dim] + k, 4)
    return tuple(out)


def dot_nn(a, b):
    return lax.dot_general(a, b, (((1,), (0,)), ((), ())), preferred_element_type=F32)


class Reduce:
    def __init__(self, p, xyz, core, g, fa, fb, fl, fr, s2, r2, s3, r3, send, recv):
        self.p, self.xyz, self.core = p, xyz, core
        self.g, self.fa, self.fb, self.fl, self.fr = g, fa, fb, fl, fr
        self.s2, self.r2, self.s3, self.r3 = s2, r2, s3, r3
        self.send, self.recv = send, recv
        self.sent = []

    def copy(self, i, src, dst, xyz):
        c = pltpu.make_async_remote_copy(
            src_ref=src, dst_ref=dst, send_sem=self.send.at[self.p, i], recv_sem=self.recv.at[self.p, i],
            device_id=device(xyz, self.core), device_id_type=MESH)
        c.start()
        self.sent.append(c)
        return c

    def at(self, k, lo, n):
        start = pl.multiple_of(lax.rem(self.xyz[ORDERS[self.p][0]] + k, 4) * 144 + lo, 16)
        return pl.ds(start, n)

    def start(self):
        p, d = self.p, ORDERS[self.p][0]
        right, left = shifted(self.xyz, d, 1), shifted(self.xyz, d, 3)
        self.c0 = self.copy(0, self.g.at[p, self.at(2, 0, RA)], self.fa.at[p], right)
        self.c1 = self.copy(1, self.g.at[p, self.at(2, RA, RB)], self.fb.at[p], left)
        self.c2 = self.copy(2, self.g.at[p, self.at(1, RA, RB)], self.fl.at[p, pl.ds(RA, RB)], right)
        self.c3 = self.copy(3, self.g.at[p, self.at(3, 0, RA)], self.fr.at[p, pl.ds(0, RA)], left)

    def forward(self):
        p, d = self.p, ORDERS[self.p][0]
        right, left = shifted(self.xyz, d, 1), shifted(self.xyz, d, 3)
        self.c0.wait_recv()
        r = self.at(1, 0, RA)
        self.g[p, r] = (self.g[p, r].astype(F32) + self.fa[p].astype(F32)).astype(BF16)
        self.c4 = self.copy(4, self.g.at[p, r], self.fl.at[p, pl.ds(0, RA)], right)
        self.c1.wait_recv()
        r = self.at(3, RA, RB)
        self.g[p, r] = (self.g[p, r].astype(F32) + self.fb[p].astype(F32)).astype(BF16)
        self.c5 = self.copy(5, self.g.at[p, r], self.fr.at[p, pl.ds(RA, RB)], left)

    def second(self, pad2):
        p, d = self.p, ORDERS[self.p][1]
        for c in (self.c2, self.c3, self.c4, self.c5):
            c.wait_recv()
        r = self.at(0, 0, 144)
        total = self.g[p, r].astype(F32) + self.fl[p].astype(F32) + self.fr[p].astype(F32)
        self.s2[p] = dot_nn(pad2[...], total.astype(BF16)).astype(BF16)
        self.cs2 = []
        for k in (2, 1, 3):
            peer = shifted(self.xyz, d, k)
            rows = pl.ds(pl.multiple_of(peer[d] * 48, 16), 48)
            self.cs2.append(self.copy(5 + k, self.s2.at[p, rows], self.r2.at[p, k - 1], peer))

    def third(self, pad3):
        p, d = self.p, ORDERS[self.p][2]
        for c in self.cs2:
            c.wait_recv()
        rows = pl.ds(pl.multiple_of(self.xyz[ORDERS[p][1]] * 48, 16), 48)
        total = self.s2[p, rows].astype(F32)
        for k in range(3):
            total = total + self.r2[p, k].astype(F32)
        self.s3[p] = dot_nn(pad3[...], total.astype(BF16)).astype(BF16)
        self.cs3 = []
        for k in (2, 1, 3):
            peer = shifted(self.xyz, d, k)
            rows = pl.ds(pl.multiple_of(peer[d] * 16, 16), 16)
            self.cs3.append(self.copy(8 + k, self.s3.at[p, rows], self.r3.at[p, k - 1], peer))

    def finish(self):
        p = self.p
        for c in self.cs3:
            c.wait_recv()
        rows = pl.ds(pl.multiple_of(self.xyz[ORDERS[p][2]] * 16, 16), 16)
        total = self.s3[p, rows].astype(F32)
        for k in range(3):
            total = total + self.r3[p, k].astype(F32)
        for c in self.sent:
            c.wait_send()
        return total[:9].astype(BF16)


def reduce_scratch():
    return [
        pltpu.VMEM((PARTS, 576, D), BF16),
        pltpu.VMEM((PARTS, RA, D), BF16),
        pltpu.VMEM((PARTS, RB, D), BF16),
        pltpu.VMEM((PARTS, 144, D), BF16),
        pltpu.VMEM((PARTS, 144, D), BF16),
        pltpu.VMEM((PARTS, 192, D), BF16),
        pltpu.VMEM((PARTS, 3, 48, D), BF16),
        pltpu.VMEM((PARTS, 64, D), BF16),
        pltpu.VMEM((PARTS, 3, 16, D), BF16),
        pltpu.SemaphoreType.DMA((PARTS, 12)),
        pltpu.SemaphoreType.DMA((PARTS, 12)),
    ]


def partners(xyz, core):
    out = [device(shifted(xyz, d, k), core) for d in range(3) for k in (1, 2, 3)]
    out.append(device(xyz, 1 - core))
    return out


def entry_barrier(devices):
    sem = pltpu.get_barrier_semaphore()
    for dev in devices:
        pl.semaphore_signal(sem, inc=1, device_id=dev, device_id_type=MESH)
    pl.semaphore_wait(sem, len(devices))


def rs_kernel(gw, pad2, pad3, outq, outo, pair, psend, precv, *scratch):
    xyz, core = coords()
    entry_barrier(partners(xyz, core))
    g = scratch[0]
    pairs = []
    for p in range(PARTS):
        other = pl.ds(pl.multiple_of((1 - core) * 576, 576), 576)
        c = pltpu.make_async_remote_copy(
            src_ref=gw.at[p, other], dst_ref=pair.at[p], send_sem=psend.at[p], recv_sem=precv.at[p],
            device_id=device(xyz, 1 - core), device_id_type=MESH)
        c.start()
        pairs.append(c)
    parts = [Reduce(p, xyz, core, *scratch) for p in range(PARTS)]
    for p in range(PARTS):
        pairs[p].wait_recv()

        def add(i, c, p=p):
            r = pl.ds(pl.multiple_of(i * 16, 16), 16)
            mine = pl.ds(pl.multiple_of(core * 576 + i * 16, 16), 16)
            g[p, r] = (gw[p, mine].astype(F32) + pair[p, r].astype(F32)).astype(BF16)
            return c

        lax.fori_loop(0, 36, add, 0)
        parts[p].start()
    for r in parts:
        r.forward()
    for r in parts:
        r.second(pad2)
    for r in parts:
        r.third(pad3)
    for p in range(3):
        outq[:, p * D:(p + 1) * D] = parts[p].finish()
    outo[...] = parts[3].finish()
    for c in pairs:
        c.wait_send()


def reduce_scatter(gw):
    vm = pl.BlockSpec(memory_space=pltpu.VMEM)
    pad2 = jnp.asarray(spread(36, 48), BF16)
    pad3 = jnp.asarray(np.pad(spread(9, 16), ((0, 0), (0, 12))), BF16)
    return pl.pallas_call(
        rs_kernel,
        out_shape=(jax.ShapeDtypeStruct((9, 3 * D), BF16), jax.ShapeDtypeStruct((9, D), BF16)),
        in_specs=[vm] * 3,
        out_specs=(vm, vm),
        scratch_shapes=[pltpu.VMEM((PARTS, 576, D), BF16), pltpu.SemaphoreType.DMA((PARTS,)),
                        pltpu.SemaphoreType.DMA((PARTS,))] + reduce_scratch(),
        compiler_params=pltpu.CompilerParams(collective_id=0, has_side_effects=True, vmem_limit_bytes=56 * 1024 * 1024),
        cost_estimate=pl.CostEstimate(flops=10**9, bytes_accessed=20 * 2**20, transcendentals=0),
    )(gw, pad2, pad3)


HD = 72
NH = 16
GR = 256
N = 512


def dot_nt(a, b):
    return lax.dot_general(a, b, (((1,), (1,)), ((), ())), preferred_element_type=F32)


def dot_tn(a, b):
    return lax.dot_general(a, b, (((0,), (0,)), ((), ())), preferred_element_type=F32)


def group_rows(g):
    if isinstance(g, int):
        return pl.ds(g * GR, GR)
    return pl.ds(pl.multiple_of(g * GR, GR), GR)


def sub_rows(g, i, n):
    return pl.ds(pl.multiple_of(g * GR + i * n, n), n)


LN_CH = 64


def ln_forward(g, tok, shift, scale, xh, rstd, hid):
    def body(i, c):
        r = sub_rows(g, i, LN_CH)
        x = tok[r, :].astype(F32)
        xc = x - jnp.mean(x, axis=-1, keepdims=True)
        rs = lax.rsqrt(jnp.mean(xc * xc, axis=-1, keepdims=True) + 1e-6)
        n = xc * rs
        xh[r, :] = n
        rstd[r, :] = jnp.broadcast_to(rs, (LN_CH, 128))
        hid[r, :] = (n * (1.0 + scale[...]) + shift[...]).astype(BF16)
        return c

    lax.fori_loop(0, GR // LN_CH, body, 0, unroll=2)


def ln_backward(g, gh, cot, scale, xh, rstd, gtok):
    def body(i, c):
        r = sub_rows(g, i, LN_CH)
        n = xh[r, :]
        gm = gh[r, :].astype(F32) * (1.0 + scale[...])
        m1 = jnp.mean(gm, axis=-1, keepdims=True)
        m2 = jnp.mean(gm * n, axis=-1, keepdims=True)
        gx = rstd[r, :1] * (gm - m1 - n * m2)
        gtok[r, :] = (cot[r, :].astype(F32) + gx).astype(BF16)
        return c

    lax.fori_loop(0, GR // LN_CH, body, 0, unroll=2)


def head_sum(x, ones_in):
    return dot_nn(x.astype(BF16), ones_in[...]) * (1.0 / HD)


def head_spread(m, ones_out):
    hi = m.astype(BF16)
    lo = (m - hi.astype(F32)).astype(BF16)
    return dot_nn(hi, ones_out[...]) + dot_nn(lo, ones_out[...])


def norm_forward(g, proj, qg, kg, qn, kn, ones_in, ones_out):
    r = group_rows(g)
    for col, gain, dst in ((0, qg, qn), (D, kg, kn)):
        x = proj[r, pl.ds(col, D)].astype(F32)
        ms = head_sum(x * x, ones_in)
        inv = head_spread(lax.rsqrt(ms + 1e-6), ones_out)
        dst[r, :] = (x * inv * gain[...]).astype(BF16)


def norm_backward(g, proj, qg, kg, dqn, dkn, ones_in, ones_out):
    r = group_rows(g)
    for col, gain, dn in ((0, qg, dqn), (D, kg, dkn)):
        x = proj[r, pl.ds(col, D)].astype(F32)
        inv = head_spread(lax.rsqrt(head_sum(x * x, ones_in) + 1e-6), ones_out)
        xh = x * inv
        d = dn[r, :].astype(F32) * gain[...]
        m = head_spread(head_sum(d * xh, ones_in), ones_out)
        proj[r, pl.ds(col, D)] = (inv * (d - xh * m)).astype(BF16)


def head_window(h):
    lo, hi = h * HD, (h + 1) * HD
    t0, t1 = lo // 128, (hi - 1) // 128
    return t0, t1 + 1, lo - t0 * 128, hi - t0 * 128


def lane_mask(lo, hi, w):
    lane = lax.broadcasted_iota(jnp.int32, (1, w), 1)
    return (lane >= lo) & (lane < hi)


def pick(x, lo, hi):
    w = x.shape[1]
    lane = lax.broadcasted_iota(jnp.int32, x.shape, 1)
    return jnp.where((lane >= lo) & (lane < hi), x, jnp.zeros_like(x))


def block_mask():
    ri = lax.broadcasted_iota(jnp.int32, (GR, GR), 0)
    ci = lax.broadcasted_iota(jnp.int32, (GR, GR), 1)
    return (ri & 15) == (ci & 15)


class Tiles:
    def __init__(self, ref, r, col):
        self.ref, self.r, self.col, self.part = ref, r, col, {}

    def add(self, h, val):
        t0, t1, lo, hi = head_window(h)
        for t in range(t0, t1):
            piece = val[:, (t - t0) * 128:(t - t0 + 1) * 128]
            if t in self.part:
                lane = lax.broadcasted_iota(jnp.int32, piece.shape, 1)
                piece = jnp.where(lane >= h * HD - t * 128, piece, self.part.pop(t))
            if (h + 1) * HD >= (t + 1) * 128:
                self.ref[self.r, pl.ds(self.col + t * 128, 128)] = piece.astype(BF16)
            else:
                self.part[t] = piece


def att_forward(g, proj, qn, kn, att, prob):
    r = group_rows(g)
    mask = block_mask()
    out = Tiles(att, r, 0)
    for h in range(NH):
        t0, t1, lo, hi = head_window(h)
        w = pl.ds(t0 * 128, (t1 - t0) * 128)
        q = pick(qn[r, w], lo, hi)
        s = dot_nt(q, kn[r, w])
        e = jnp.where(mask, jnp.exp(s), 0.0)
        p = (e * (1.0 / jnp.sum(e, axis=-1, keepdims=True))).astype(BF16)
        prob[g, h] = p
        out.add(h, dot_nn(p, proj[r, pl.ds(2 * D + t0 * 128, (t1 - t0) * 128)]))


def att_backward(g, proj, qn, kn, att, gatt, prob, ones_in):
    r = group_rows(g)
    delta = head_sum(gatt[r, :].astype(F32) * att[r, :].astype(F32) * HD, ones_in)
    odq, odk, odv = Tiles(qn, r, 0), Tiles(kn, r, 0), Tiles(proj, r, 2 * D)
    for h in range(NH):
        t0, t1, lo, hi = head_window(h)
        w = pl.ds(t0 * 128, (t1 - t0) * 128)
        da = gatt[r, w]
        q, k = qn[r, w], kn[r, w]
        dp = dot_nt(pick(da, lo, hi), proj[r, pl.ds(2 * D + t0 * 128, (t1 - t0) * 128)])
        p = prob[g, h]
        ds = (p.astype(F32) * (dp - delta[:, h:h + 1])).astype(BF16)
        odv.add(h, dot_tn(p, da))
        odq.add(h, dot_nn(ds, k))
        odk.add(h, dot_tn(ds, q))


def out_projection(g, tok, att, wo, gate, out):
    r = group_rows(g)
    out[r, :] = (tok[r, :].astype(F32) + gate[...] * dot_nn(att[r, :], wo[...])).astype(BF16)


def grad_att(g, cot, gate, wo, gp, gatt):
    r = group_rows(g)
    x = (cot[r, :].astype(F32) * gate[...]).astype(BF16)
    gp[r, :] = x
    gatt[r, :] = dot_nt(x, wo[...]).astype(BF16)


PCH = 192


def permuted_t(p, x, idx, xt):
    def body(i, c):
        r = pl.ds(pl.multiple_of(i * PCH, PCH), PCH)
        lane = lax.broadcasted_iota(jnp.int32, (PCH, D), 1)
        m = jnp.where(idx[r, p:p + 1] == lane, 1.0, 0.0).astype(BF16)
        xt[r, :] = dot_nt(m, x[...]).astype(BF16)
        return c

    lax.fori_loop(0, D // PCH, body, 0)


def solo_kernel(tok, cot, shift, scale, gate, wqkv, wo, qg, kg, idx, ones_in, ones_out, out, gtok, gw,
                hid, xh, rstd, proj, qn, kn, att, prob, gp, gatt, xt):
    for g in range(2):
        ln_forward(g, tok, shift, scale, xh, rstd, hid)
        r = group_rows(g)
    for b in range(3):
        cs = pl.ds(b * D, D)
        proj[:, cs] = dot_nn(hid[...], wqkv[:, cs]).astype(BF16)
    for g in range(2):
        norm_forward(g, proj, qg, kg, qn, kn, ones_in, ones_out)

    def fwd(g, c):
        att_forward(g, proj, qn, kn, att, prob)
        return c

    lax.fori_loop(0, 2, fwd, 0)
    for g in range(2):
        out_projection(g, tok, att, wo, gate, out)
        grad_att(g, cot, gate, wo, gp, gatt)

    permuted_t(3, att, idx, xt)
    gw[3] = dot_nn(xt[...], gp[...]).astype(BF16)

    def bwd(g, c):
        att_backward(g, proj, qn, kn, att, gatt, prob, ones_in)
        return c

    lax.fori_loop(0, 2, bwd, 0)
    for g in range(2):
        norm_backward(g, proj, qg, kg, qn, kn, ones_in, ones_out)
    for b in range(3):
        permuted_t(b, hid, idx, xt)
        gw[b] = dot_nn(xt[...], proj[:, pl.ds(b * D, D)]).astype(BF16)
    gatt[...] = dot_nt(proj[...], wqkv[...]).astype(BF16)
    for g in range(2):
        ln_backward(g, gatt, cot, scale, xh, rstd, gtok)


def ones_matrices():
    a = np.zeros((D, 128), np.float32)
    b = np.zeros((128, D), np.float32)
    for h in range(NH):
        a[h * HD:(h + 1) * HD, h] = 1.0
        b[h, h * HD:(h + 1) * HD] = 1.0
    return a, b


def compute(tok, cot, shift, scale, gate, wqkv, wo, qg, kg):
    vm = pl.BlockSpec(memory_space=pltpu.VMEM)
    a, b = ones_matrices()
    qgf = jnp.tile(qg * HD ** -0.5, (1, NH))
    kgf = jnp.tile(kg, (1, NH))
    return pl.pallas_call(
        solo_kernel,
        out_shape=(
            jax.ShapeDtypeStruct((N, D), BF16),
            jax.ShapeDtypeStruct((N, D), BF16),
            jax.ShapeDtypeStruct((4, D, D), BF16),
        ),
        in_specs=[vm] * 12,
        out_specs=(vm,) * 3,
        scratch_shapes=[
            pltpu.VMEM((N, D), BF16),
            pltpu.VMEM((N, D), F32),
            pltpu.VMEM((N, 128), F32),
            pltpu.VMEM((N, 3 * D), BF16),
            pltpu.VMEM((N, D), BF16),
            pltpu.VMEM((N, D), BF16),
            pltpu.VMEM((N, D), BF16),
            pltpu.VMEM((2, NH, GR, GR), BF16),
            pltpu.VMEM((N, D), BF16),
            pltpu.VMEM((N, D), BF16),
            pltpu.VMEM((D, N), BF16),
        ],
        compiler_params=pltpu.CompilerParams(vmem_limit_bytes=62 * 1024 * 1024),
    )(tok, cot, shift, scale, gate, wqkv, wo, qgf, kgf, jnp.asarray(natural_rows()),
      jnp.asarray(a, BF16), jnp.asarray(b, BF16))


def to_groups(x):
    y = lax.all_to_all(x[0], "seq", split_axis=1, concat_axis=0, tiled=True)
    f, p, d = y.shape
    return y.reshape(f, p // 16, 16, d).transpose(1, 0, 2, 3).reshape(f * p, d)


def from_groups(y, frames, pos):
    z = y.reshape(pos // 16, frames, 16, D).transpose(1, 0, 2, 3).reshape(frames, pos, D)
    return lax.all_to_all(z, "seq", split_axis=0, concat_axis=1, tiled=True)[None]


def on_device(tokens, mod_shift, mod_scale, res_gate, qkv_weight, out_weight, query_gain, key_gain, cotangent):
    tok = to_groups(tokens)
    cot = to_groups(cotangent)
    n = tok.shape[0]
    out, gtok, gw = compute(tok, cot, mod_shift, mod_scale, res_gate, qkv_weight, out_weight,
                            query_gain[None], key_gain[None])
    block_output = from_groups(out, 16, n // 16)
    grad_tokens = from_groups(gtok, 16, n // 16)
    grad_qkv_weight, grad_out_weight = reduce_scatter(gw)
    return block_output, grad_tokens, grad_qkv_weight, grad_out_weight


def solution(mesh):
    tok = P("dp", "seq", None, None)
    vec = P("dp", None)
    return jax.shard_map(
        on_device,
        mesh=mesh,
        in_specs=(tok, vec, vec, vec, P(), P(), P(), P(), tok),
        out_specs=(tok, tok, P(("dp", "seq"), None), P(("dp", "seq"), None)),
        check_vma=False,
    )
```

```python
import numpy as np
import jax
import jax.numpy as jnp
from jax import lax
from jax.experimental import pallas as pl
from jax.experimental.pallas import tpu as pltpu
from jax.sharding import PartitionSpec as P

F32 = jnp.float32
BF16 = jnp.bfloat16
D = 1152
MESH = pl.DeviceIdType.MESH
PARTS = 4
ORDERS = ((1, 0, 2), (0, 2, 1), (2, 1, 0), (1, 2, 0))
RA, RB = 80, 64


def natural_rows():
    i = np.arange(D)
    core, rest = i // 576, i % 576
    a = (rest // 144, (rest // 36) % 4, (rest // 9) % 4)
    j = rest % 9
    table = np.zeros((D, PARTS), np.int32)
    for p, order in enumerate(ORDERS):
        c = [None] * 3
        for place, dim in enumerate(order):
            c[dim] = a[place]
        x, y, z = c
        table[:, p] = 9 * ((z % 2) * 64 + y * 16 + core * 8 + x * 2 + z // 2) + j
    return table


def spread(rows_from, rows_to):
    m = np.zeros((4 * rows_to, 4 * rows_from), np.float32)
    for b in range(4):
        for j in range(rows_from):
            m[b * rows_to + j, b * rows_from + j] = 1.0
    return m


def coords():
    dp = lax.axis_index("dp")
    sq = lax.axis_index("seq")
    z = lax.rem(sq, 2) * 2 + dp // 8
    return (sq // 2, lax.rem(dp // 2, 4), z), lax.rem(dp, 2)


def device(xyz, core):
    x, y, z = xyz
    return (lax.rem(z, 2) * 8 + y * 2 + core, x * 2 + z // 2)


def shifted(xyz, dim, k):
    out = list(xyz)
    out[dim] = lax.rem(xyz[dim] + k, 4)
    return tuple(out)


def dot_nn(a, b):
    return lax.dot_general(a, b, (((1,), (0,)), ((), ())), preferred_element_type=F32)


class Reduce:
    def __init__(self, p, xyz, core, g, fa, fb, fl, fr, s2, r2, s3, r3, send, recv):
        self.p, self.xyz, self.core = p, xyz, core
        self.g, self.fa, self.fb, self.fl, self.fr = g, fa, fb, fl, fr
        self.s2, self.r2, self.s3, self.r3 = s2, r2, s3, r3
        self.send, self.recv = send, recv
        self.sent = []

    def copy(self, i, src, dst, xyz):
        c = pltpu.make_async_remote_copy(
            src_ref=src, dst_ref=dst, send_sem=self.send.at[self.p, i], recv_sem=self.recv.at[self.p, i],
            device_id=device(xyz, self.core), device_id_type=MESH)
        c.start()
        self.sent.append(c)
        return c

    def at(self, k, lo, n):
        start = pl.multiple_of(lax.rem(self.xyz[ORDERS[self.p][0]] + k, 4) * 144 + lo, 16)
        return pl.ds(start, n)

    def start(self):
        p, d = self.p, ORDERS[self.p][0]
        right, left = shifted(self.xyz, d, 1), shifted(self.xyz, d, 3)
        self.c0 = self.copy(0, self.g.at[p, self.at(2, 0, RA)], self.fa.at[p], right)
        self.c1 = self.copy(1, self.g.at[p, self.at(2, RA, RB)], self.fb.at[p], left)
        self.c2 = self.copy(2, self.g.at[p, self.at(1, RA, RB)], self.fl.at[p, pl.ds(RA, RB)], right)
        self.c3 = self.copy(3, self.g.at[p, self.at(3, 0, RA)], self.fr.at[p, pl.ds(0, RA)], left)

    def forward(self):
        p, d = self.p, ORDERS[self.p][0]
        right, left = shifted(self.xyz, d, 1), shifted(self.xyz, d, 3)
        self.c0.wait_recv()
        r = self.at(1, 0, RA)
        self.g[p, r] = (self.g[p, r].astype(F32) + self.fa[p].astype(F32)).astype(BF16)
        self.c4 = self.copy(4, self.g.at[p, r], self.fl.at[p, pl.ds(0, RA)], right)
        self.c1.wait_recv()
        r = self.at(3, RA, RB)
        self.g[p, r] = (self.g[p, r].astype(F32) + self.fb[p].astype(F32)).astype(BF16)
        self.c5 = self.copy(5, self.g.at[p, r], self.fr.at[p, pl.ds(RA, RB)], left)

    def second(self, pad2):
        p, d = self.p, ORDERS[self.p][1]
        for c in (self.c2, self.c3, self.c4, self.c5):
            c.wait_recv()
        r = self.at(0, 0, 144)
        total = self.g[p, r].astype(F32) + self.fl[p].astype(F32) + self.fr[p].astype(F32)
        self.s2[p] = dot_nn(pad2[...], total.astype(BF16)).astype(BF16)
        self.cs2 = []
        for k in (2, 1, 3):
            peer = shifted(self.xyz, d, k)
            rows = pl.ds(pl.multiple_of(peer[d] * 48, 16), 48)
            self.cs2.append(self.copy(5 + k, self.s2.at[p, rows], self.r2.at[p, k - 1], peer))

    def third(self, pad3):
        p, d = self.p, ORDERS[self.p][2]
        for c in self.cs2:
            c.wait_recv()
        rows = pl.ds(pl.multiple_of(self.xyz[ORDERS[p][1]] * 48, 16), 48)
        total = self.s2[p, rows].astype(F32)
        for k in range(3):
            total = total + self.r2[p, k].astype(F32)
        self.s3[p] = dot_nn(pad3[...], total.astype(BF16)).astype(BF16)
        self.cs3 = []
        for k in (2, 1, 3):
            peer = shifted(self.xyz, d, k)
            rows = pl.ds(pl.multiple_of(peer[d] * 16, 16), 16)
            self.cs3.append(self.copy(8 + k, self.s3.at[p, rows], self.r3.at[p, k - 1], peer))

    def finish(self):
        p = self.p
        for c in self.cs3:
            c.wait_recv()
        rows = pl.ds(pl.multiple_of(self.xyz[ORDERS[p][2]] * 16, 16), 16)
        total = self.s3[p, rows].astype(F32)
        for k in range(3):
            total = total + self.r3[p, k].astype(F32)
        for c in self.sent:
            c.wait_send()
        return total[:9].astype(BF16)


def reduce_scratch():
    return [
        pltpu.VMEM((PARTS, 576, D), BF16),
        pltpu.VMEM((PARTS, RA, D), BF16),
        pltpu.VMEM((PARTS, RB, D), BF16),
        pltpu.VMEM((PARTS, 144, D), BF16),
        pltpu.VMEM((PARTS, 144, D), BF16),
        pltpu.VMEM((PARTS, 192, D), BF16),
        pltpu.VMEM((PARTS, 3, 48, D), BF16),
        pltpu.VMEM((PARTS, 64, D), BF16),
        pltpu.VMEM((PARTS, 3, 16, D), BF16),
        pltpu.SemaphoreType.DMA((PARTS, 12)),
        pltpu.SemaphoreType.DMA((PARTS, 12)),
    ]


HD = 72
NH = 16
GR = 256
N = 512


def dot_nt(a, b):
    return lax.dot_general(a, b, (((1,), (1,)), ((), ())), preferred_element_type=F32)


def dot_tn(a, b):
    return lax.dot_general(a, b, (((0,), (0,)), ((), ())), preferred_element_type=F32)


def group_rows(g):
    if isinstance(g, int):
        return pl.ds(g * GR, GR)
    return pl.ds(pl.multiple_of(g * GR, GR), GR)


def sub_rows(g, i, n):
    return pl.ds(pl.multiple_of(g * GR + i * n, n), n)


LN_CH = 64
FCH = LN_CH // 16


def frames(i):
    return pl.ds(i * FCH, FCH)


def frame_rows(ref, g, i):
    return ref[g, frames(i)].reshape(LN_CH, D)


def ln_forward(g, tok, shift, scale, xh, rstd, hid):
    def body(i, c):
        r = sub_rows(g, i, LN_CH)
        x = frame_rows(tok, g, i).astype(F32)
        xc = x - jnp.mean(x, axis=-1, keepdims=True)
        rs = lax.rsqrt(jnp.mean(xc * xc, axis=-1, keepdims=True) + 1e-6)
        n = xc * rs
        xh[r, :] = n
        rstd[r, :] = jnp.broadcast_to(rs, (LN_CH, 128))
        hid[r, :] = (n * (1.0 + scale[...]) + shift[...]).astype(BF16)
        return c

    lax.fori_loop(0, GR // LN_CH, body, 0, unroll=2)


def ln_backward(g, gh, cot, scale, xh, rstd, gtok):
    def body(i, c):
        r = sub_rows(g, i, LN_CH)
        n = xh[r, :]
        gm = gh[r, :].astype(F32) * (1.0 + scale[...])
        m1 = jnp.mean(gm, axis=-1, keepdims=True)
        m2 = jnp.mean(gm * n, axis=-1, keepdims=True)
        gx = rstd[r, :1] * (gm - m1 - n * m2)
        gtok[g, frames(i)] = (frame_rows(cot, g, i).astype(F32) + gx).astype(BF16).reshape(FCH, 16, D)
        return c

    lax.fori_loop(0, GR // LN_CH, body, 0, unroll=2)


def head_sum(x, ones_in):
    return dot_nn(x.astype(BF16), ones_in[...]) * (1.0 / HD)


def head_spread(m, ones_out):
    hi = m.astype(BF16)
    lo = (m - hi.astype(F32)).astype(BF16)
    return dot_nn(hi, ones_out[...]) + dot_nn(lo, ones_out[...])


def norm_forward(g, proj, qg, kg, qn, kn, ones_in, ones_out):
    r = group_rows(g)
    for col, gain, dst in ((0, qg, qn), (D, kg, kn)):
        x = proj[r, pl.ds(col, D)].astype(F32)
        ms = head_sum(x * x, ones_in)
        inv = head_spread(lax.rsqrt(ms + 1e-6), ones_out)
        dst[r, :] = (x * inv * gain[...]).astype(BF16)


def norm_backward(g, proj, qg, kg, dqn, dkn, ones_in, ones_out):
    r = group_rows(g)
    for col, gain, dn in ((0, qg, dqn), (D, kg, dkn)):
        x = proj[r, pl.ds(col, D)].astype(F32)
        inv = head_spread(lax.rsqrt(head_sum(x * x, ones_in) + 1e-6), ones_out)
        xh = x * inv
        d = dn[r, :].astype(F32) * gain[...]
        m = head_spread(head_sum(d * xh, ones_in), ones_out)
        proj[r, pl.ds(col, D)] = (inv * (d - xh * m)).astype(BF16)


def head_window(h):
    lo, hi = h * HD, (h + 1) * HD
    t0, t1 = lo // 128, (hi - 1) // 128
    return t0, t1 + 1, lo - t0 * 128, hi - t0 * 128


def lane_mask(lo, hi, w):
    lane = lax.broadcasted_iota(jnp.int32, (1, w), 1)
    return (lane >= lo) & (lane < hi)


def pick(x, lo, hi):
    w = x.shape[1]
    lane = lax.broadcasted_iota(jnp.int32, x.shape, 1)
    return jnp.where((lane >= lo) & (lane < hi), x, jnp.zeros_like(x))


def block_mask():
    ri = lax.broadcasted_iota(jnp.int32, (GR, GR), 0)
    ci = lax.broadcasted_iota(jnp.int32, (GR, GR), 1)
    return (ri & 15) == (ci & 15)


class Tiles:
    def __init__(self, ref, r, col):
        self.ref, self.r, self.col, self.part = ref, r, col, {}

    def add(self, h, val):
        t0, t1, lo, hi = head_window(h)
        for t in range(t0, t1):
            piece = val[:, (t - t0) * 128:(t - t0 + 1) * 128]
            if t in self.part:
                lane = lax.broadcasted_iota(jnp.int32, piece.shape, 1)
                piece = jnp.where(lane >= h * HD - t * 128, piece, self.part.pop(t))
            if (h + 1) * HD >= (t + 1) * 128:
                self.ref[self.r, pl.ds(self.col + t * 128, 128)] = piece.astype(BF16)
            else:
                self.part[t] = piece


def att_forward(g, proj, qn, kn, att, prob):
    r = group_rows(g)
    mask = block_mask()
    out = Tiles(att, r, 0)
    for h in range(NH):
        t0, t1, lo, hi = head_window(h)
        w = pl.ds(t0 * 128, (t1 - t0) * 128)
        q = pick(qn[r, w], lo, hi)
        s = dot_nt(q, kn[r, w])
        e = jnp.where(mask, jnp.exp(s), 0.0)
        p = (e * (1.0 / jnp.sum(e, axis=-1, keepdims=True))).astype(BF16)
        prob[g, h] = p
        out.add(h, dot_nn(p, proj[r, pl.ds(2 * D + t0 * 128, (t1 - t0) * 128)]))


def att_backward(g, proj, qn, kn, att, gatt, prob, ones_in):
    r = group_rows(g)
    delta = head_sum(gatt[r, :].astype(F32) * att[r, :].astype(F32) * HD, ones_in)
    odq, odk, odv = Tiles(qn, r, 0), Tiles(kn, r, 0), Tiles(proj, r, 2 * D)
    for h in range(NH):
        t0, t1, lo, hi = head_window(h)
        w = pl.ds(t0 * 128, (t1 - t0) * 128)
        da = gatt[r, w]
        q, k = qn[r, w], kn[r, w]
        dp = dot_nt(pick(da, lo, hi), proj[r, pl.ds(2 * D + t0 * 128, (t1 - t0) * 128)])
        p = prob[g, h]
        ds = (p.astype(F32) * (dp - delta[:, h:h + 1])).astype(BF16)
        odv.add(h, dot_tn(p, da))
        odq.add(h, dot_nn(ds, k))
        odk.add(h, dot_tn(ds, q))


def out_projection(g, tok, att, wo, gate, out):
    r = group_rows(g)
    y = tok[g].reshape(GR, D).astype(F32) + gate[...] * dot_nn(att[r, :], wo[...])
    out[g] = y.astype(BF16).reshape(16, 16, D)


def grad_att(g, cot, gate, wo, gp, gatt):
    r = group_rows(g)
    x = (cot[g].reshape(GR, D).astype(F32) * gate[...]).astype(BF16)
    gp[r, :] = x
    gatt[r, :] = dot_nt(x, wo[...]).astype(BF16)


def permuted_t(p, x, idx, xt):
    def body(i, c):
        r = pl.ds(pl.multiple_of(i * 576, 64), 576)
        lane = lax.broadcasted_iota(jnp.int32, (576, D), 1)
        m = jnp.where(idx[r, p:p + 1] == lane, 1.0, 0.0).astype(BF16)
        xt[p, r, :] = dot_nt(m, x[...]).astype(BF16)
        return c

    lax.fori_loop(0, 2, body, 0)


class Exchange:
    def __init__(self, a, send, recv, local, seq, dp):
        self.a, self.send, self.recv, self.local, self.seq, self.dp = a, send, recv, local, seq, dp

    def refs(self, g, peer):
        raise NotImplementedError

    def remote(self, g, k):
        peer = lax.rem(self.seq + k, 8)
        src, dst = self.refs(g, peer)
        return pltpu.make_async_remote_copy(
            src_ref=src, dst_ref=dst, send_sem=self.send.at[self.a, g, k], recv_sem=self.recv.at[self.a, g, k],
            device_id=(self.dp, peer), device_id_type=MESH)

    def own(self, g):
        src, dst = self.refs(g, self.seq)
        return pltpu.make_async_copy(src, dst, self.local.at[self.a, g])

    def start(self, g):
        for k in (1, 2, 3, 4, 5, 6, 7):
            self.remote(g, k).start()
        self.own(g).start()

    def arrive(self, g):
        for k in (1, 2, 3, 4, 5, 6, 7):
            self.remote(g, k).wait_recv()
        self.own(g).wait()

    def leave(self, g):
        for k in (1, 2, 3, 4, 5, 6, 7):
            self.remote(g, k).wait_send()


class Inward(Exchange):
    def __init__(self, src, dst, *rest):
        super().__init__(*rest)
        self.src, self.dst = src, dst

    def refs(self, g, peer):
        rows = pl.ds(pl.multiple_of(peer * 32 + g * 16, 16), 16)
        return self.src.at[0, :, rows, :], self.dst.at[g, pl.ds(self.seq * 2, 2)]


class Outward(Inward):
    def refs(self, g, peer):
        rows = pl.ds(pl.multiple_of(self.seq * 32 + g * 16, 16), 16)
        return self.src.at[g, pl.ds(peer * 2, 2)], self.dst.at[0, :, rows, :]


def partners(xyz, core):
    out = [device(shifted(xyz, d, k), core) for d in range(3) for k in (1, 2, 3)]
    out.append(device(xyz, 1 - core))
    far = shifted(xyz, 2, 2)
    out.extend(device(shifted(far, 0, k), core) for k in (1, 2, 3))
    return out


def entry_barrier(devices):
    sem = pltpu.get_barrier_semaphore()
    for dev in devices:
        pl.semaphore_signal(sem, inc=1, device_id=dev, device_id_type=MESH)
    pl.semaphore_wait(sem, len(devices))


def half(core):
    return pl.ds(pl.multiple_of(core * 576, 64), 576)


def kernel(tok_h, cot_h, wqkv_h, wo_h, shift, scale, gate, qg, kg, idx, ones_in, ones_out, pad2, pad3,
           out_h, gtok_h, outq, outo,
           tok, cot, wqkv, wo, hid, xh, rstd, proj, qn, kn, att, prob, gp, gatt, xt, out,
           pout, pin, wsem, isend, irecv, ilocal, osend, orecv, olocal, psend, precv, *scratch):
    g_ref = scratch[0]
    cw = pltpu.make_async_copy(wqkv_h, wqkv, wsem.at[0])
    co = pltpu.make_async_copy(wo_h, wo, wsem.at[1])
    cw.start()
    co.start()
    xyz, core = coords()
    dp, sq = lax.axis_index("dp"), lax.axis_index("seq")
    entry_barrier(partners(xyz, core))
    tok_in = Inward(tok_h, tok, 0, isend, irecv, ilocal, sq, dp)
    cot_in = Inward(cot_h, cot, 1, isend, irecv, ilocal, sq, dp)
    block_out = Outward(out, out_h, 0, osend, orecv, olocal, sq, dp)
    gtok_out = Outward(tok, gtok_h, 1, osend, orecv, olocal, sq, dp)
    for x in (tok_in, cot_in):
        for g in range(2):
            x.start(g)
    parts = [Reduce(p, xyz, core, *scratch) for p in range(PARTS)]
    cw.wait()
    co.wait()

    def forward(g, c):
        tok_in.arrive(g)
        ln_forward(g, tok, shift, scale, xh, rstd, hid)
        r = group_rows(g)
        for b in range(3):
            cs = pl.ds(b * D, D)
            proj[r, cs] = dot_nn(hid[r, :], wqkv[:, cs]).astype(BF16)
        norm_forward(g, proj, qg, kg, qn, kn, ones_in, ones_out)
        att_forward(g, proj, qn, kn, att, prob)
        out_projection(g, tok, att, wo, gate, out)
        block_out.start(g)
        return c

    lax.fori_loop(0, 2, forward, 0)
    permuted_t(3, att, idx, xt)
    for p in range(3):
        permuted_t(p, hid, idx, xt)

    def gradient(g, c):
        cot_in.arrive(g)
        grad_att(g, cot, gate, wo, gp, gatt)
        return c

    lax.fori_loop(0, 2, gradient, 0)

    def pair(p):
        return pltpu.make_async_remote_copy(
            src_ref=pout.at[p % 3], dst_ref=pin.at[p], send_sem=psend.at[p], recv_sem=precv.at[p],
            device_id=device(xyz, 1 - core), device_id_type=MESH)

    def weight(p, right):
        pout[p % 3] = dot_nn(xt[p, half(1 - core), :], right[...]).astype(BF16)
        pair(p).start()
        g_ref[p] = dot_nn(xt[p, half(core), :], right[...]).astype(BF16)

    def reduce(p):
        pair(p).wait_recv()

        def add(i, c):
            r = pl.ds(pl.multiple_of(i * 48, 16), 48)
            g_ref[p, r] = (g_ref[p, r].astype(F32) + pin[p, r].astype(F32)).astype(BF16)
            return c

        lax.fori_loop(0, 12, add, 0)
        parts[p].start()

    weight(3, gp)
    pair(3).wait_send()
    reduce(3)

    def backward(g, c):
        att_backward(g, proj, qn, kn, att, gatt, prob, ones_in)
        norm_backward(g, proj, qg, kg, qn, kn, ones_in, ones_out)
        return c

    lax.fori_loop(0, 2, backward, 0)
    parts[3].forward()
    weight(2, proj.at[:, pl.ds(2 * D, D)])
    weight(0, proj.at[:, pl.ds(0, D)])
    reduce(2)
    weight(1, proj.at[:, pl.ds(D, D)])
    reduce(0)
    parts[3].second(pad2)
    reduce(1)

    def leave(g, c):
        r = group_rows(g)
        gatt[r, :] = dot_nt(proj[r, :], wqkv[...]).astype(BF16)
        ln_backward(g, gatt, cot, scale, xh, rstd, tok)
        gtok_out.start(g)
        return c

    lax.fori_loop(0, 2, leave, 0)
    for p in (2, 0, 1):
        parts[p].forward()
    parts[3].third(pad3)
    for p in (2, 0, 1):
        parts[p].second(pad2)
    outo[...] = parts[3].finish()
    for p in (2, 0, 1):
        parts[p].third(pad3)
    for p in (2, 0, 1):
        outq[:, p * D:(p + 1) * D] = parts[p].finish()
    for p in range(3):
        pair(p).wait_send()
    for x in (tok_in, cot_in):
        for g in range(2):
            x.leave(g)
    for x in (block_out, gtok_out):
        for g in range(2):
            x.arrive(g)
            x.leave(g)


def ones_matrices():
    a = np.zeros((D, 128), np.float32)
    b = np.zeros((128, D), np.float32)
    for h in range(NH):
        a[h * HD:(h + 1) * HD, h] = 1.0
        b[h, h * HD:(h + 1) * HD] = 1.0
    return jnp.asarray(a, BF16), jnp.asarray(b, BF16)


def on_device(tokens, mod_shift, mod_scale, res_gate, qkv_weight, out_weight, query_gain, key_gain, cotangent):
    vm = pl.BlockSpec(memory_space=pltpu.VMEM)
    anywhere = pl.BlockSpec(memory_space=pl.ANY)
    ones_in, ones_out = ones_matrices()
    pad2 = jnp.asarray(spread(36, 48), BF16)
    pad3 = jnp.asarray(np.pad(spread(9, 16), ((0, 0), (0, 12))), BF16)
    qg = jnp.tile(query_gain[None] * HD ** -0.5, (1, NH))
    kg = jnp.tile(key_gain[None], (1, NH))
    dma = pltpu.SemaphoreType.DMA
    return pl.pallas_call(
        kernel,
        out_shape=(
            jax.ShapeDtypeStruct(tokens.shape, BF16),
            jax.ShapeDtypeStruct(tokens.shape, BF16),
            jax.ShapeDtypeStruct((9, 3 * D), BF16),
            jax.ShapeDtypeStruct((9, D), BF16),
        ),
        in_specs=[anywhere] * 4 + [vm] * 10,
        out_specs=(anywhere, anywhere, vm, vm),
        scratch_shapes=[
            pltpu.VMEM((2, 16, 16, D), BF16),
            pltpu.VMEM((2, 16, 16, D), BF16),
            pltpu.VMEM((D, 3 * D), BF16),
            pltpu.VMEM((D, D), BF16),
            pltpu.VMEM((N, D), BF16),
            pltpu.VMEM((N, D), F32),
            pltpu.VMEM((N, 128), F32),
            pltpu.VMEM((N, 3 * D), BF16),
            pltpu.VMEM((N, D), BF16),
            pltpu.VMEM((N, D), BF16),
            pltpu.VMEM((N, D), BF16),
            pltpu.VMEM((2, NH, GR, GR), BF16),
            pltpu.VMEM((N, D), BF16),
            pltpu.VMEM((N, D), BF16),
            pltpu.VMEM((PARTS, D, N), BF16),
            pltpu.VMEM((2, 16, 16, D), BF16),
            pltpu.VMEM((3, 576, D), BF16),
            pltpu.VMEM((PARTS, 576, D), BF16),
            dma((2,)),
            dma((2, 2, 8)), dma((2, 2, 8)), dma((2, 2)),
            dma((2, 2, 8)), dma((2, 2, 8)), dma((2, 2)),
            dma((PARTS,)), dma((PARTS,)),
        ] + reduce_scratch(),
        compiler_params=pltpu.CompilerParams(collective_id=0, has_side_effects=True,
                                             vmem_limit_bytes=63 * 1024 * 1024),
        cost_estimate=pl.CostEstimate(flops=18 * 10**9, bytes_accessed=16 * 2**20, transcendentals=2**21),
    )(tokens, cotangent, qkv_weight, out_weight, mod_shift, mod_scale, res_gate, qg, kg,
      jnp.asarray(natural_rows()), ones_in, ones_out, pad2, pad3)


def solution(mesh):
    tok = P("dp", "seq", None, None)
    vec = P("dp", None)
    return jax.shard_map(
        on_device,
        mesh=mesh,
        in_specs=(tok, vec, vec, vec, P(), P(), P(), P(), tok),
        out_specs=(tok, tok, P(("dp", "seq"), None), P(("dp", "seq"), None)),
        check_vma=False,
    )
```

```python
import numpy as np
import jax
import jax.numpy as jnp
from jax import lax
from jax.experimental import pallas as pl
from jax.experimental.pallas import tpu as pltpu
from jax.sharding import PartitionSpec as P

F32 = jnp.float32
BF16 = jnp.bfloat16
D = 1152
MESH = pl.DeviceIdType.MESH
PARTS = 4
ORDERS = ((1, 0, 2), (0, 2, 1), (2, 1, 0), (1, 2, 0))
RA, RB = 80, 64


def natural_rows():
    i = np.arange(D)
    core, rest = i // 576, i % 576
    a = (rest // 144, (rest // 36) % 4, (rest // 9) % 4)
    j = rest % 9
    table = np.zeros((D, PARTS), np.int32)
    for p, order in enumerate(ORDERS):
        c = [None] * 3
        for place, dim in enumerate(order):
            c[dim] = a[place]
        x, y, z = c
        table[:, p] = 9 * ((z % 2) * 64 + y * 16 + core * 8 + x * 2 + z // 2) + j
    return table


def spread(rows_from, rows_to):
    m = np.zeros((4 * rows_to, 4 * rows_from), np.float32)
    for b in range(4):
        for j in range(rows_from):
            m[b * rows_to + j, b * rows_from + j] = 1.0
    return m


def coords():
    dp = lax.axis_index("dp")
    sq = lax.axis_index("seq")
    z = lax.rem(sq, 2) * 2 + dp // 8
    return (sq // 2, lax.rem(dp // 2, 4), z), lax.rem(dp, 2)


def device(xyz, core):
    x, y, z = xyz
    return (lax.rem(z, 2) * 8 + y * 2 + core, x * 2 + z // 2)


def shifted(xyz, dim, k):
    out = list(xyz)
    out[dim] = lax.rem(xyz[dim] + k, 4)
    return tuple(out)


def dot_nn(a, b):
    return lax.dot_general(a, b, (((1,), (0,)), ((), ())), preferred_element_type=F32)


class Reduce:
    def __init__(self, p, xyz, core, g, fa, fb, fl, fr, s2, r2, s3, r3, send, recv):
        self.p, self.xyz, self.core = p, xyz, core
        self.g, self.fa, self.fb, self.fl, self.fr = g, fa, fb, fl, fr
        self.s2, self.r2, self.s3, self.r3 = s2, r2, s3, r3
        self.send, self.recv = send, recv
        self.sent = []

    def copy(self, i, src, dst, xyz):
        c = pltpu.make_async_remote_copy(
            src_ref=src, dst_ref=dst, send_sem=self.send.at[self.p, i], recv_sem=self.recv.at[self.p, i],
            device_id=device(xyz, self.core), device_id_type=MESH)
        c.start()
        self.sent.append(c)
        return c

    def at(self, k, lo, n):
        start = pl.multiple_of(lax.rem(self.xyz[ORDERS[self.p][0]] + k, 4) * 144 + lo, 16)
        return pl.ds(start, n)

    def start(self):
        p, d = self.p, ORDERS[self.p][0]
        right, left = shifted(self.xyz, d, 1), shifted(self.xyz, d, 3)
        self.c0 = self.copy(0, self.g.at[p, self.at(2, 0, RA)], self.fa.at[p], right)
        self.c1 = self.copy(1, self.g.at[p, self.at(2, RA, RB)], self.fb.at[p], left)
        self.c2 = self.copy(2, self.g.at[p, self.at(1, RA, RB)], self.fl.at[p, pl.ds(RA, RB)], right)
        self.c3 = self.copy(3, self.g.at[p, self.at(3, 0, RA)], self.fr.at[p, pl.ds(0, RA)], left)

    def forward(self):
        p, d = self.p, ORDERS[self.p][0]
        right, left = shifted(self.xyz, d, 1), shifted(self.xyz, d, 3)
        self.c0.wait_recv()
        r = self.at(1, 0, RA)
        self.g[p, r] = (self.g[p, r].astype(F32) + self.fa[p].astype(F32)).astype(BF16)
        self.c4 = self.copy(4, self.g.at[p, r], self.fl.at[p, pl.ds(0, RA)], right)
        self.c1.wait_recv()
        r = self.at(3, RA, RB)
        self.g[p, r] = (self.g[p, r].astype(F32) + self.fb[p].astype(F32)).astype(BF16)
        self.c5 = self.copy(5, self.g.at[p, r], self.fr.at[p, pl.ds(RA, RB)], left)

    def second(self, pad2):
        p, d = self.p, ORDERS[self.p][1]
        for c in (self.c2, self.c3, self.c4, self.c5):
            c.wait_recv()
        r = self.at(0, 0, 144)
        total = self.g[p, r].astype(F32) + self.fl[p].astype(F32) + self.fr[p].astype(F32)
        self.s2[p] = dot_nn(pad2[...], total.astype(BF16)).astype(BF16)
        self.cs2 = []
        for k in (2, 1, 3):
            peer = shifted(self.xyz, d, k)
            rows = pl.ds(pl.multiple_of(peer[d] * 48, 16), 48)
            self.cs2.append(self.copy(5 + k, self.s2.at[p, rows], self.r2.at[p, k - 1], peer))

    def third(self, pad3):
        p, d = self.p, ORDERS[self.p][2]
        for c in self.cs2:
            c.wait_recv()
        rows = pl.ds(pl.multiple_of(self.xyz[ORDERS[p][1]] * 48, 16), 48)
        total = self.s2[p, rows].astype(F32)
        for k in range(3):
            total = total + self.r2[p, k].astype(F32)
        self.s3[p] = dot_nn(pad3[...], total.astype(BF16)).astype(BF16)
        self.cs3 = []
        for k in (2, 1, 3):
            peer = shifted(self.xyz, d, k)
            rows = pl.ds(pl.multiple_of(peer[d] * 16, 16), 16)
            self.cs3.append(self.copy(8 + k, self.s3.at[p, rows], self.r3.at[p, k - 1], peer))

    def finish(self):
        p = self.p
        for c in self.cs3:
            c.wait_recv()
        rows = pl.ds(pl.multiple_of(self.xyz[ORDERS[p][2]] * 16, 16), 16)
        total = self.s3[p, rows].astype(F32)
        for k in range(3):
            total = total + self.r3[p, k].astype(F32)
        for c in self.sent:
            c.wait_send()
        return total[:9].astype(BF16)


def reduce_scratch():
    return [
        pltpu.VMEM((PARTS, 576, D), BF16),
        pltpu.VMEM((PARTS, RA, D), BF16),
        pltpu.VMEM((PARTS, RB, D), BF16),
        pltpu.VMEM((PARTS, 144, D), BF16),
        pltpu.VMEM((PARTS, 144, D), BF16),
        pltpu.VMEM((PARTS, 192, D), BF16),
        pltpu.VMEM((PARTS, 3, 48, D), BF16),
        pltpu.VMEM((PARTS, 64, D), BF16),
        pltpu.VMEM((PARTS, 3, 16, D), BF16),
        pltpu.SemaphoreType.DMA((PARTS, 12)),
        pltpu.SemaphoreType.DMA((PARTS, 12)),
    ]


HD = 72
NH = 16
GR = 256
N = 512


def dot_nt(a, b):
    return lax.dot_general(a, b, (((1,), (1,)), ((), ())), preferred_element_type=F32)


def dot_tn(a, b):
    return lax.dot_general(a, b, (((0,), (0,)), ((), ())), preferred_element_type=F32)


def group_rows(g):
    if isinstance(g, int):
        return pl.ds(g * GR, GR)
    return pl.ds(pl.multiple_of(g * GR, GR), GR)


def sub_rows(g, i, n):
    return pl.ds(pl.multiple_of(g * GR + i * n, n), n)


LN_CH = 64
FCH = LN_CH // 16


def frames(i):
    return pl.ds(i * FCH, FCH)


def frame_rows(ref, g, i):
    return ref[g, frames(i)].reshape(LN_CH, D)


def ln_forward(g, tok, shift, scale, xh, rstd, hid):
    def body(i, c):
        r = sub_rows(g, i, LN_CH)
        x = frame_rows(tok, g, i).astype(F32)
        xc = x - jnp.mean(x, axis=-1, keepdims=True)
        rs = lax.rsqrt(jnp.mean(xc * xc, axis=-1, keepdims=True) + 1e-6)
        n = xc * rs
        xh[r, :] = n
        rstd[r, :] = jnp.broadcast_to(rs, (LN_CH, 128))
        hid[r, :] = (n * (1.0 + scale[...]) + shift[...]).astype(BF16)
        return c

    lax.fori_loop(0, GR // LN_CH, body, 0, unroll=2)


def ln_backward(g, gh, cot, scale, xh, rstd, gtok):
    def body(i, c):
        r = sub_rows(g, i, 16)
        n = xh[r, :]
        gm = gh[r, :].astype(F32) * (1.0 + scale[...])
        m1 = jnp.mean(gm, axis=-1, keepdims=True)
        m2 = jnp.mean(gm * n, axis=-1, keepdims=True)
        gx = rstd[r, :1] * (gm - m1 - n * m2)
        gtok[g, i] = (cot[g, i].astype(F32) + gx).astype(BF16)
        return c

    lax.fori_loop(0, 16, body, 0, unroll=4)


def head_sum(x, ones_in):
    return dot_nn(x.astype(BF16), ones_in[...]) * (1.0 / HD)


def head_spread(m, ones_out):
    hi = m.astype(BF16)
    lo = (m - hi.astype(F32)).astype(BF16)
    return dot_nn(hi, ones_out[...]) + dot_nn(lo, ones_out[...])


def norm_forward(g, proj, qg, kg, qn, kn, ones_in, ones_out):
    r = group_rows(g)
    for col, gain, dst in ((0, qg, qn), (D, kg, kn)):
        x = proj[r, pl.ds(col, D)].astype(F32)
        ms = head_sum(x * x, ones_in)
        inv = head_spread(lax.rsqrt(ms + 1e-6), ones_out)
        dst[r, :] = (x * inv * gain[...]).astype(BF16)


def norm_backward(g, proj, qg, kg, dqn, dkn, ones_in, ones_out):
    r = group_rows(g)
    for col, gain, dn in ((0, qg, dqn), (D, kg, dkn)):
        x = proj[r, pl.ds(col, D)].astype(F32)
        inv = head_spread(lax.rsqrt(head_sum(x * x, ones_in) + 1e-6), ones_out)
        xh = x * inv
        d = dn[r, :].astype(F32) * gain[...]
        m = head_spread(head_sum(d * xh, ones_in), ones_out)
        proj[r, pl.ds(col, D)] = (inv * (d - xh * m)).astype(BF16)


def head_window(h):
    lo, hi = h * HD, (h + 1) * HD
    t0, t1 = lo // 128, (hi - 1) // 128
    return t0, t1 + 1, lo - t0 * 128, hi - t0 * 128


def lane_mask(lo, hi, w):
    lane = lax.broadcasted_iota(jnp.int32, (1, w), 1)
    return (lane >= lo) & (lane < hi)


def pick(x, lo, hi):
    w = x.shape[1]
    lane = lax.broadcasted_iota(jnp.int32, x.shape, 1)
    return jnp.where((lane >= lo) & (lane < hi), x, jnp.zeros_like(x))


def block_mask():
    ri = lax.broadcasted_iota(jnp.int32, (GR, GR), 0)
    ci = lax.broadcasted_iota(jnp.int32, (GR, GR), 1)
    return (ri & 15) == (ci & 15)


class Tiles:
    def __init__(self, ref, r, col):
        self.ref, self.r, self.col, self.part = ref, r, col, {}

    def add(self, h, val):
        t0, t1, lo, hi = head_window(h)
        for t in range(t0, t1):
            piece = val[:, (t - t0) * 128:(t - t0 + 1) * 128]
            if t in self.part:
                lane = lax.broadcasted_iota(jnp.int32, piece.shape, 1)
                piece = jnp.where(lane >= h * HD - t * 128, piece, self.part.pop(t))
            if (h + 1) * HD >= (t + 1) * 128:
                self.ref[self.r, pl.ds(self.col + t * 128, 128)] = piece.astype(BF16)
            else:
                self.part[t] = piece


def att_forward(g, proj, qn, kn, att, prob):
    r = group_rows(g)
    mask = block_mask()
    out = Tiles(att, r, 0)
    for h in range(NH):
        t0, t1, lo, hi = head_window(h)
        w = pl.ds(t0 * 128, (t1 - t0) * 128)
        q = pick(qn[r, w], lo, hi)
        s = dot_nt(q, kn[r, w])
        e = jnp.where(mask, jnp.exp(s), 0.0)
        p = (e * (1.0 / jnp.sum(e, axis=-1, keepdims=True))).astype(BF16)
        prob[g, h] = p
        out.add(h, dot_nn(p, proj[r, pl.ds(2 * D + t0 * 128, (t1 - t0) * 128)]))


def att_backward(g, proj, qn, kn, att, gatt, prob, ones_in):
    r = group_rows(g)
    delta = head_sum(gatt[r, :].astype(F32) * att[r, :].astype(F32) * HD, ones_in)
    odq, odk, odv = Tiles(qn, r, 0), Tiles(kn, r, 0), Tiles(proj, r, 2 * D)
    for h in range(NH):
        t0, t1, lo, hi = head_window(h)
        w = pl.ds(t0 * 128, (t1 - t0) * 128)
        da = gatt[r, w]
        q, k = qn[r, w], kn[r, w]
        dp = dot_nt(pick(da, lo, hi), proj[r, pl.ds(2 * D + t0 * 128, (t1 - t0) * 128)])
        p = prob[g, h]
        ds = (p.astype(F32) * (dp - delta[:, h:h + 1])).astype(BF16)
        odv.add(h, dot_tn(p, da))
        odq.add(h, dot_nn(ds, k))
        odk.add(h, dot_tn(ds, q))


def out_projection(g, tok, att, wo, gate, out):
    r = group_rows(g)
    y = tok[g].reshape(GR, D).astype(F32) + gate[...] * dot_nn(att[r, :], wo[...])
    out[g] = y.astype(BF16).reshape(16, 16, D)


def grad_att(g, cot, gate, wo, gp, gatt):
    r = group_rows(g)
    x = (cot[g].reshape(GR, D).astype(F32) * gate[...]).astype(BF16)
    gp[r, :] = x
    gatt[r, :] = dot_nt(x, wo[...]).astype(BF16)


def permuted_t(p, x, idx, xt):
    def body(i, c):
        r = pl.ds(pl.multiple_of(i * 576, 64), 576)
        lane = lax.broadcasted_iota(jnp.int32, (576, D), 1)
        m = jnp.where(idx[r, p:p + 1] == lane, 1.0, 0.0).astype(BF16)
        xt[p, r, :] = dot_nt(m, x[...]).astype(BF16)
        return c

    lax.fori_loop(0, 2, body, 0)


class Exchange:
    def __init__(self, a, send, recv, local, seq, dp):
        self.a, self.send, self.recv, self.local, self.seq, self.dp = a, send, recv, local, seq, dp

    def refs(self, g, peer):
        raise NotImplementedError

    def remote(self, g, k):
        peer = lax.rem(self.seq + k, 8)
        src, dst = self.refs(g, peer)
        return pltpu.make_async_remote_copy(
            src_ref=src, dst_ref=dst, send_sem=self.send.at[self.a, g, k], recv_sem=self.recv.at[self.a, g, k],
            device_id=(self.dp, peer), device_id_type=MESH)

    def own(self, g):
        src, dst = self.refs(g, self.seq)
        return pltpu.make_async_copy(src, dst, self.local.at[self.a, g])

    def start(self, g):
        for k in (1, 2, 3, 4, 5, 6, 7):
            self.remote(g, k).start()
        self.own(g).start()

    def arrive(self, g):
        for k in (1, 2, 3, 4, 5, 6, 7):
            self.remote(g, k).wait_recv()
        self.own(g).wait()

    def leave(self, g):
        for k in (1, 2, 3, 4, 5, 6, 7):
            self.remote(g, k).wait_send()


class Inward(Exchange):
    def __init__(self, src, dst, *rest):
        super().__init__(*rest)
        self.src, self.dst = src, dst

    def refs(self, g, peer):
        rows = pl.ds(pl.multiple_of(peer * 32 + g * 16, 16), 16)
        return self.src.at[0, :, rows, :], self.dst.at[g, pl.ds(self.seq * 2, 2)]


class Outward(Inward):
    def refs(self, g, peer):
        rows = pl.ds(pl.multiple_of(self.seq * 32 + g * 16, 16), 16)
        return self.src.at[g, pl.ds(peer * 2, 2)], self.dst.at[0, :, rows, :]


def partners(xyz, core):
    out = [device(shifted(xyz, d, k), core) for d in range(3) for k in (1, 2, 3)]
    out.append(device(xyz, 1 - core))
    far = shifted(xyz, 2, 2)
    out.extend(device(shifted(far, 0, k), core) for k in (1, 2, 3))
    return out


def entry_barrier(devices):
    sem = pltpu.get_barrier_semaphore()
    for dev in devices:
        pl.semaphore_signal(sem, inc=1, device_id=dev, device_id_type=MESH)
    pl.semaphore_wait(sem, len(devices))


def half(core):
    return pl.ds(pl.multiple_of(core * 576, 64), 576)


def kernel(tok_h, cot_h, wqkv_h, wo_h, shift, scale, gate, qg_h, kg_h, idx, ones_in, ones_out, pad2, pad3,
           out_h, gtok_h, outq, outo,
           tok, cot, wqkv, wo, hid, xh, rstd, proj, qn, kn, att, prob, gp, gatt, xt, out,
           pout, pin, wsem, qg, kg, isend, irecv, ilocal, osend, orecv, olocal, psend, precv, *scratch):
    g_ref = scratch[0]
    cw = pltpu.make_async_copy(wqkv_h, wqkv, wsem.at[0])
    co = pltpu.make_async_copy(wo_h, wo, wsem.at[1])
    cw.start()
    co.start()
    for h in range(NH):
        qg[:, pl.ds(h * HD, HD)] = qg_h[...] * HD ** -0.5
        kg[:, pl.ds(h * HD, HD)] = kg_h[...]
    xyz, core = coords()
    dp, sq = lax.axis_index("dp"), lax.axis_index("seq")
    entry_barrier(partners(xyz, core))
    tok_in = Inward(tok_h, tok, 0, isend, irecv, ilocal, sq, dp)
    cot_in = Inward(cot_h, cot, 1, isend, irecv, ilocal, sq, dp)
    block_out = Outward(out, out_h, 0, osend, orecv, olocal, sq, dp)
    gtok_out = Outward(tok, gtok_h, 1, osend, orecv, olocal, sq, dp)
    for x in (tok_in, cot_in):
        for g in range(2):
            x.start(g)
    parts = [Reduce(p, xyz, core, *scratch) for p in range(PARTS)]
    cw.wait()
    co.wait()

    def forward(g, c):
        tok_in.arrive(g)
        ln_forward(g, tok, shift, scale, xh, rstd, hid)
        r = group_rows(g)
        for b in range(3):
            cs = pl.ds(b * D, D)
            proj[r, cs] = dot_nn(hid[r, :], wqkv[:, cs]).astype(BF16)
        norm_forward(g, proj, qg, kg, qn, kn, ones_in, ones_out)
        att_forward(g, proj, qn, kn, att, prob)
        out_projection(g, tok, att, wo, gate, out)
        block_out.start(g)
        return c

    lax.fori_loop(0, 2, forward, 0)
    permuted_t(3, att, idx, xt)
    for p in range(3):
        permuted_t(p, hid, idx, xt)

    def gradient(g, c):
        cot_in.arrive(g)
        grad_att(g, cot, gate, wo, gp, gatt)
        return c

    lax.fori_loop(0, 2, gradient, 0)

    def pair(p):
        return pltpu.make_async_remote_copy(
            src_ref=pout.at[p % 3], dst_ref=pin.at[p], send_sem=psend.at[p], recv_sem=precv.at[p],
            device_id=device(xyz, 1 - core), device_id_type=MESH)

    def weight(p, right):
        pout[p % 3] = dot_nn(xt[p, half(1 - core), :], right[...]).astype(BF16)
        pair(p).start()
        g_ref[p] = dot_nn(xt[p, half(core), :], right[...]).astype(BF16)

    def reduce(p):
        pair(p).wait_recv()

        def add(i, c):
            r = pl.ds(pl.multiple_of(i * 48, 16), 48)
            g_ref[p, r] = (g_ref[p, r].astype(F32) + pin[p, r].astype(F32)).astype(BF16)
            return c

        lax.fori_loop(0, 12, add, 0)
        parts[p].start()

    weight(3, gp)
    pair(3).wait_send()
    reduce(3)

    def backward(g, c):
        att_backward(g, proj, qn, kn, att, gatt, prob, ones_in)
        norm_backward(g, proj, qg, kg, qn, kn, ones_in, ones_out)
        return c

    lax.fori_loop(0, 2, backward, 0)
    parts[3].forward()
    weight(2, proj.at[:, pl.ds(2 * D, D)])
    weight(0, proj.at[:, pl.ds(0, D)])
    reduce(2)
    weight(1, proj.at[:, pl.ds(D, D)])
    reduce(0)
    parts[3].second(pad2)
    reduce(1)

    def leave(g, c):
        r = group_rows(g)
        gatt[r, :] = dot_nt(proj[r, :], wqkv[...]).astype(BF16)
        ln_backward(g, gatt, cot, scale, xh, rstd, tok)
        gtok_out.start(g)
        return c

    lax.fori_loop(0, 2, leave, 0)
    for p in (2, 0, 1):
        parts[p].forward()
    parts[3].third(pad3)
    for p in (2, 0, 1):
        parts[p].second(pad2)
    outo[...] = parts[3].finish()
    for p in (2, 0, 1):
        parts[p].third(pad3)
    for p in (2, 0, 1):
        outq[:, p * D:(p + 1) * D] = parts[p].finish()
    for p in range(3):
        pair(p).wait_send()
    for x in (tok_in, cot_in):
        for g in range(2):
            x.leave(g)
    for x in (block_out, gtok_out):
        for g in range(2):
            x.arrive(g)
            x.leave(g)


def ones_matrices():
    a = np.zeros((D, 128), np.float32)
    b = np.zeros((128, D), np.float32)
    for h in range(NH):
        a[h * HD:(h + 1) * HD, h] = 1.0
        b[h, h * HD:(h + 1) * HD] = 1.0
    return jnp.asarray(a, BF16), jnp.asarray(b, BF16)


def on_device(tokens, mod_shift, mod_scale, res_gate, qkv_weight, out_weight, query_gain, key_gain, cotangent):
    vm = pl.BlockSpec(memory_space=pltpu.VMEM)
    anywhere = pl.BlockSpec(memory_space=pl.ANY)
    ones_in, ones_out = ones_matrices()
    pad2 = jnp.asarray(spread(36, 48), BF16)
    pad3 = jnp.asarray(np.pad(spread(9, 16), ((0, 0), (0, 12))), BF16)
    dma = pltpu.SemaphoreType.DMA
    return pl.pallas_call(
        kernel,
        out_shape=(
            jax.ShapeDtypeStruct(tokens.shape, BF16),
            jax.ShapeDtypeStruct(tokens.shape, BF16),
            jax.ShapeDtypeStruct((9, 3 * D), BF16),
            jax.ShapeDtypeStruct((9, D), BF16),
        ),
        in_specs=[anywhere] * 4 + [vm] * 10,
        out_specs=(anywhere, anywhere, vm, vm),
        scratch_shapes=[
            pltpu.VMEM((2, 16, 16, D), BF16),
            pltpu.VMEM((2, 16, 16, D), BF16),
            pltpu.VMEM((D, 3 * D), BF16),
            pltpu.VMEM((D, D), BF16),
            pltpu.VMEM((N, D), BF16),
            pltpu.VMEM((N, D), F32),
            pltpu.VMEM((N, 128), F32),
            pltpu.VMEM((N, 3 * D), BF16),
            pltpu.VMEM((N, D), BF16),
            pltpu.VMEM((N, D), BF16),
            pltpu.VMEM((N, D), BF16),
            pltpu.VMEM((2, NH, GR, GR), BF16),
            pltpu.VMEM((N, D), BF16),
            pltpu.VMEM((N, D), BF16),
            pltpu.VMEM((PARTS, D, N), BF16),
            pltpu.VMEM((2, 16, 16, D), BF16),
            pltpu.VMEM((3, 576, D), BF16),
            pltpu.VMEM((PARTS, 576, D), BF16),
            dma((2,)),
            pltpu.VMEM((1, D), F32), pltpu.VMEM((1, D), F32),
            dma((2, 2, 8)), dma((2, 2, 8)), dma((2, 2)),
            dma((2, 2, 8)), dma((2, 2, 8)), dma((2, 2)),
            dma((PARTS,)), dma((PARTS,)),
        ] + reduce_scratch(),
        compiler_params=pltpu.CompilerParams(collective_id=0, has_side_effects=True,
                                             vmem_limit_bytes=63 * 1024 * 1024),
        cost_estimate=pl.CostEstimate(flops=18 * 10**9, bytes_accessed=16 * 2**20, transcendentals=2**21),
    )(tokens, cotangent, qkv_weight, out_weight, mod_shift, mod_scale, res_gate, query_gain[None], key_gain[None],
      jnp.asarray(natural_rows()), ones_in, ones_out, pad2, pad3)


def solution(mesh):
    tok = P("dp", "seq", None, None)
    vec = P("dp", None)
    return jax.shard_map(
        on_device,
        mesh=mesh,
        in_specs=(tok, vec, vec, vec, P(), P(), P(), P(), tok),
        out_specs=(tok, tok, P(("dp", "seq"), None), P(("dp", "seq"), None)),
        check_vma=False,
    )
```

```python
import numpy as np
import jax
import jax.numpy as jnp
from jax import lax
from jax.experimental import pallas as pl
from jax.experimental.pallas import tpu as pltpu
from jax.sharding import PartitionSpec as P

F32 = jnp.float32
BF16 = jnp.bfloat16
D = 1152
MESH = pl.DeviceIdType.MESH
PARTS = 4
ORDERS = ((1, 0, 2), (0, 2, 1), (2, 1, 0), (1, 2, 0))
RA, RB = 80, 64


def natural_rows():
    i = np.arange(D)
    core, rest = i // 576, i % 576
    a = (rest // 144, (rest // 36) % 4, (rest // 9) % 4)
    j = rest % 9
    table = np.zeros((D, PARTS), np.int32)
    for p, order in enumerate(ORDERS):
        c = [None] * 3
        for place, dim in enumerate(order):
            c[dim] = a[place]
        x, y, z = c
        table[:, p] = 9 * ((z % 2) * 64 + y * 16 + core * 8 + x * 2 + z // 2) + j
    return table


def spread(rows_from, rows_to):
    m = np.zeros((4 * rows_to, 4 * rows_from), np.float32)
    for b in range(4):
        for j in range(rows_from):
            m[b * rows_to + j, b * rows_from + j] = 1.0
    return m


def coords():
    dp = lax.axis_index("dp")
    sq = lax.axis_index("seq")
    z = lax.rem(sq, 2) * 2 + dp // 8
    return (sq // 2, lax.rem(dp // 2, 4), z), lax.rem(dp, 2)


def device(xyz, core):
    x, y, z = xyz
    return (lax.rem(z, 2) * 8 + y * 2 + core, x * 2 + z // 2)


def shifted(xyz, dim, k):
    out = list(xyz)
    out[dim] = lax.rem(xyz[dim] + k, 4)
    return tuple(out)


def dot_nn(a, b):
    return lax.dot_general(a, b, (((1,), (0,)), ((), ())), preferred_element_type=F32)


class Reduce:
    def __init__(self, p, xyz, core, g, fa, fb, fl, fr, s2, r2, s3, r3, send, recv):
        self.p, self.xyz, self.core = p, xyz, core
        self.g, self.fa, self.fb, self.fl, self.fr = g, fa, fb, fl, fr
        self.s2, self.r2, self.s3, self.r3 = s2, r2, s3, r3
        self.send, self.recv = send, recv
        self.sent = []

    def copy(self, i, src, dst, xyz):
        c = pltpu.make_async_remote_copy(
            src_ref=src, dst_ref=dst, send_sem=self.send.at[self.p, i], recv_sem=self.recv.at[self.p, i],
            device_id=device(xyz, self.core), device_id_type=MESH)
        c.start()
        self.sent.append(c)
        return c

    def at(self, k, lo, n):
        start = pl.multiple_of(lax.rem(self.xyz[ORDERS[self.p][0]] + k, 4) * 144 + lo, 16)
        return pl.ds(start, n)

    def start(self):
        p, d = self.p, ORDERS[self.p][0]
        right, left = shifted(self.xyz, d, 1), shifted(self.xyz, d, 3)
        self.c0 = self.copy(0, self.g.at[p, self.at(2, 0, RA)], self.fa.at[p], right)
        self.c1 = self.copy(1, self.g.at[p, self.at(2, RA, RB)], self.fb.at[p], left)
        self.c2 = self.copy(2, self.g.at[p, self.at(1, RA, RB)], self.fl.at[p, pl.ds(RA, RB)], right)
        self.c3 = self.copy(3, self.g.at[p, self.at(3, 0, RA)], self.fr.at[p, pl.ds(0, RA)], left)

    def forward(self):
        p, d = self.p, ORDERS[self.p][0]
        right, left = shifted(self.xyz, d, 1), shifted(self.xyz, d, 3)
        self.c0.wait_recv()
        r = self.at(1, 0, RA)
        self.g[p, r] = (self.g[p, r].astype(F32) + self.fa[p].astype(F32)).astype(BF16)
        self.c4 = self.copy(4, self.g.at[p, r], self.fl.at[p, pl.ds(0, RA)], right)
        self.c1.wait_recv()
        r = self.at(3, RA, RB)
        self.g[p, r] = (self.g[p, r].astype(F32) + self.fb[p].astype(F32)).astype(BF16)
        self.c5 = self.copy(5, self.g.at[p, r], self.fr.at[p, pl.ds(RA, RB)], left)

    def second(self, pad2):
        p, d = self.p, ORDERS[self.p][1]
        for c in (self.c2, self.c3, self.c4, self.c5):
            c.wait_recv()
        r = self.at(0, 0, 144)
        total = self.g[p, r].astype(F32) + self.fl[p].astype(F32) + self.fr[p].astype(F32)
        self.s2[p] = dot_nn(pad2[...], total.astype(BF16)).astype(BF16)
        self.cs2 = []
        for k in (2, 1, 3):
            peer = shifted(self.xyz, d, k)
            rows = pl.ds(pl.multiple_of(peer[d] * 48, 16), 48)
            self.cs2.append(self.copy(5 + k, self.s2.at[p, rows], self.r2.at[p, k - 1], peer))

    def third(self, pad3):
        p, d = self.p, ORDERS[self.p][2]
        for c in self.cs2:
            c.wait_recv()
        rows = pl.ds(pl.multiple_of(self.xyz[ORDERS[p][1]] * 48, 16), 48)
        total = self.s2[p, rows].astype(F32)
        for k in range(3):
            total = total + self.r2[p, k].astype(F32)
        self.s3[p] = dot_nn(pad3[...], total.astype(BF16)).astype(BF16)
        self.cs3 = []
        for k in (2, 1, 3):
            peer = shifted(self.xyz, d, k)
            rows = pl.ds(pl.multiple_of(peer[d] * 16, 16), 16)
            self.cs3.append(self.copy(8 + k, self.s3.at[p, rows], self.r3.at[p, k - 1], peer))

    def finish(self):
        p = self.p
        for c in self.cs3:
            c.wait_recv()
        rows = pl.ds(pl.multiple_of(self.xyz[ORDERS[p][2]] * 16, 16), 16)
        total = self.s3[p, rows].astype(F32)
        for k in range(3):
            total = total + self.r3[p, k].astype(F32)
        for c in self.sent:
            c.wait_send()
        return total[:9].astype(BF16)


def reduce_scratch():
    return [
        pltpu.VMEM((PARTS, 576, D), BF16),
        pltpu.VMEM((PARTS, RA, D), BF16),
        pltpu.VMEM((PARTS, RB, D), BF16),
        pltpu.VMEM((PARTS, 144, D), BF16),
        pltpu.VMEM((PARTS, 144, D), BF16),
        pltpu.VMEM((PARTS, 192, D), BF16),
        pltpu.VMEM((PARTS, 3, 48, D), BF16),
        pltpu.VMEM((PARTS, 64, D), BF16),
        pltpu.VMEM((PARTS, 3, 16, D), BF16),
        pltpu.SemaphoreType.DMA((PARTS, 12)),
        pltpu.SemaphoreType.DMA((PARTS, 12)),
    ]


HD = 72
NH = 16
GR = 256
N = 512


def dot_nt(a, b):
    return lax.dot_general(a, b, (((1,), (1,)), ((), ())), preferred_element_type=F32)


def dot_tn(a, b):
    return lax.dot_general(a, b, (((0,), (0,)), ((), ())), preferred_element_type=F32)


def group_rows(g):
    if isinstance(g, int):
        return pl.ds(g * GR, GR)
    return pl.ds(pl.multiple_of(g * GR, GR), GR)


def sub_rows(g, i, n):
    return pl.ds(pl.multiple_of(g * GR + i * n, n), n)


LN_CH = 64
FCH = LN_CH // 16


def frames(i):
    return pl.ds(i * FCH, FCH)


def frame_rows(ref, g, i):
    return ref[g, frames(i)].reshape(LN_CH, D)


def ln_forward(g, tok, shift, scale, xh, rstd, hid):
    def body(i, c):
        r = sub_rows(g, i, LN_CH)
        x = frame_rows(tok, g, i).astype(F32)
        xc = x - jnp.mean(x, axis=-1, keepdims=True)
        rs = lax.rsqrt(jnp.mean(xc * xc, axis=-1, keepdims=True) + 1e-6)
        n = xc * rs
        xh[r, :] = n
        rstd[r, :] = jnp.broadcast_to(rs, (LN_CH, 128))
        hid[r, :] = (n * (1.0 + scale[...]) + shift[...]).astype(BF16)
        return c

    lax.fori_loop(0, GR // LN_CH, body, 0, unroll=2)


def ln_backward(g, gh, cot, scale, xh, rstd, gtok):
    def body(i, c):
        r = sub_rows(g, i, 16)
        n = xh[r, :]
        gm = gh[r, :].astype(F32) * (1.0 + scale[...])
        m1 = jnp.mean(gm, axis=-1, keepdims=True)
        m2 = jnp.mean(gm * n, axis=-1, keepdims=True)
        gx = rstd[r, :1] * (gm - m1 - n * m2)
        gtok[g, i] = (cot[g, i].astype(F32) + gx).astype(BF16)
        return c

    lax.fori_loop(0, 16, body, 0, unroll=4)


def head_sum(x, ones_in):
    return dot_nn(x.astype(BF16), ones_in[...]) * (1.0 / HD)


def head_spread(m, ones_out):
    hi = m.astype(BF16)
    lo = (m - hi.astype(F32)).astype(BF16)
    return dot_nn(jnp.concatenate([hi, lo], axis=1), ones_out[...])


def norm_forward(g, proj, qg, kg, qn, kn, ones_in, ones_out):
    r = group_rows(g)
    for col, gain, dst in ((0, qg, qn), (D, kg, kn)):
        x = proj[r, pl.ds(col, D)].astype(F32)
        ms = head_sum(x * x, ones_in)
        inv = head_spread(lax.rsqrt(ms + 1e-6), ones_out)
        dst[r, :] = (x * inv * gain[...]).astype(BF16)


def norm_backward(g, proj, qg, kg, dqn, dkn, ones_in, ones_out):
    r = group_rows(g)
    for col, gain, dn in ((0, qg, dqn), (D, kg, dkn)):
        x = proj[r, pl.ds(col, D)].astype(F32)
        inv = head_spread(lax.rsqrt(head_sum(x * x, ones_in) + 1e-6), ones_out)
        xh = x * inv
        d = dn[r, :].astype(F32) * gain[...]
        m = head_spread(head_sum(d * xh, ones_in), ones_out)
        proj[r, pl.ds(col, D)] = (inv * (d - xh * m)).astype(BF16)


def head_window(h):
    lo, hi = h * HD, (h + 1) * HD
    t0, t1 = lo // 128, (hi - 1) // 128
    return t0, t1 + 1, lo - t0 * 128, hi - t0 * 128


def lane_mask(lo, hi, w):
    lane = lax.broadcasted_iota(jnp.int32, (1, w), 1)
    return (lane >= lo) & (lane < hi)


def pick(x, lo, hi):
    w = x.shape[1]
    lane = lax.broadcasted_iota(jnp.int32, x.shape, 1)
    return jnp.where((lane >= lo) & (lane < hi), x, jnp.zeros_like(x))


def block_mask():
    ri = lax.broadcasted_iota(jnp.int32, (GR, GR), 0)
    ci = lax.broadcasted_iota(jnp.int32, (GR, GR), 1)
    return (ri & 15) == (ci & 15)


class Tiles:
    def __init__(self, ref, r, col):
        self.ref, self.r, self.col, self.part = ref, r, col, {}

    def add(self, h, val):
        t0, t1, lo, hi = head_window(h)
        for t in range(t0, t1):
            piece = val[:, (t - t0) * 128:(t - t0 + 1) * 128]
            if t in self.part:
                lane = lax.broadcasted_iota(jnp.int32, piece.shape, 1)
                piece = jnp.where(lane >= h * HD - t * 128, piece, self.part.pop(t))
            if (h + 1) * HD >= (t + 1) * 128:
                self.ref[self.r, pl.ds(self.col + t * 128, 128)] = piece.astype(BF16)
            else:
                self.part[t] = piece


def att_forward(g, proj, qn, kn, att, prob):
    r = group_rows(g)
    mask = block_mask()
    out = Tiles(att, r, 0)
    for h in range(NH):
        t0, t1, lo, hi = head_window(h)
        w = pl.ds(t0 * 128, (t1 - t0) * 128)
        q = pick(qn[r, w], lo, hi)
        s = dot_nt(q, kn[r, w])
        e = jnp.where(mask, jnp.exp(s), 0.0)
        p = (e * (1.0 / jnp.sum(e, axis=-1, keepdims=True))).astype(BF16)
        prob[g, h] = p
        out.add(h, dot_nn(p, proj[r, pl.ds(2 * D + t0 * 128, (t1 - t0) * 128)]))


def att_backward(g, proj, qn, kn, att, gatt, prob, ones_in):
    r = group_rows(g)
    delta = head_sum(gatt[r, :].astype(F32) * att[r, :].astype(F32) * HD, ones_in)
    odq, odk, odv = Tiles(qn, r, 0), Tiles(kn, r, 0), Tiles(proj, r, 2 * D)
    for h in range(NH):
        t0, t1, lo, hi = head_window(h)
        w = pl.ds(t0 * 128, (t1 - t0) * 128)
        da = gatt[r, w]
        q, k = qn[r, w], kn[r, w]
        dp = dot_nt(pick(da, lo, hi), proj[r, pl.ds(2 * D + t0 * 128, (t1 - t0) * 128)])
        p = prob[g, h]
        ds = (p.astype(F32) * (dp - delta[:, h:h + 1])).astype(BF16)
        odv.add(h, dot_tn(p, da))
        odq.add(h, dot_nn(ds, k))
        odk.add(h, dot_tn(ds, q))


def out_projection(g, tok, att, wo, gate, out):
    r = group_rows(g)
    y = tok[g].reshape(GR, D).astype(F32) + gate[...] * dot_nn(att[r, :], wo[...])
    out[g] = y.astype(BF16).reshape(16, 16, D)


def grad_att(g, cot, gate, wo, gp, gatt):
    r = group_rows(g)
    x = (cot[g].reshape(GR, D).astype(F32) * gate[...]).astype(BF16)
    gp[r, :] = x
    gatt[r, :] = dot_nt(x, wo[...]).astype(BF16)


def permuted_t(p, x, idx, xt):
    def body(i, c):
        r = pl.ds(pl.multiple_of(i * 576, 64), 576)
        lane = lax.broadcasted_iota(jnp.int32, (576, D), 1)
        m = jnp.where(idx[r, p:p + 1] == lane, 1.0, 0.0).astype(BF16)
        xt[p, r, :] = dot_nt(m, x[...]).astype(BF16)
        return c

    lax.fori_loop(0, 2, body, 0)


class Exchange:
    def __init__(self, a, send, recv, local, seq, dp):
        self.a, self.send, self.recv, self.local, self.seq, self.dp = a, send, recv, local, seq, dp

    def refs(self, g, peer):
        raise NotImplementedError

    def remote(self, g, k):
        peer = lax.rem(self.seq + k, 8)
        src, dst = self.refs(g, peer)
        return pltpu.make_async_remote_copy(
            src_ref=src, dst_ref=dst, send_sem=self.send.at[self.a, g, k], recv_sem=self.recv.at[self.a, g, k],
            device_id=(self.dp, peer), device_id_type=MESH)

    def own(self, g):
        src, dst = self.refs(g, self.seq)
        return pltpu.make_async_copy(src, dst, self.local.at[self.a, g])

    def start(self, g):
        for k in (1, 2, 3, 4, 5, 6, 7):
            self.remote(g, k).start()
        self.own(g).start()

    def arrive(self, g):
        for k in (1, 2, 3, 4, 5, 6, 7):
            self.remote(g, k).wait_recv()
        self.own(g).wait()

    def leave(self, g):
        for k in (1, 2, 3, 4, 5, 6, 7):
            self.remote(g, k).wait_send()


class Inward(Exchange):
    def __init__(self, src, dst, *rest):
        super().__init__(*rest)
        self.src, self.dst = src, dst

    def refs(self, g, peer):
        rows = pl.ds(pl.multiple_of(peer * 32 + g * 16, 16), 16)
        return self.src.at[0, :, rows, :], self.dst.at[g, pl.ds(self.seq * 2, 2)]


class Outward(Inward):
    def refs(self, g, peer):
        rows = pl.ds(pl.multiple_of(self.seq * 32 + g * 16, 16), 16)
        return self.src.at[g, pl.ds(peer * 2, 2)], self.dst.at[0, :, rows, :]


def partners(xyz, core):
    out = [device(shifted(xyz, d, k), core) for d in range(3) for k in (1, 2, 3)]
    out.append(device(xyz, 1 - core))
    far = shifted(xyz, 2, 2)
    out.extend(device(shifted(far, 0, k), core) for k in (1, 2, 3))
    return out


def entry_barrier(devices):
    sem = pltpu.get_barrier_semaphore()
    for dev in devices:
        pl.semaphore_signal(sem, inc=1, device_id=dev, device_id_type=MESH)
    pl.semaphore_wait(sem, len(devices))


def half(core):
    return pl.ds(pl.multiple_of(core * 576, 64), 576)


def kernel(tok_h, cot_h, wqkv_h, wo_h, shift, scale, gate, qg_h, kg_h, idx, ones_in, ones_out, pad2, pad3,
           out_h, gtok_h, outq, outo,
           tok, cot, wqkv, wo, hid, xh, rstd, proj, qn, kn, att, prob, gp, gatt, xt, out,
           pout, pin, wsem, qg, kg, isend, irecv, ilocal, osend, orecv, olocal, psend, precv, *scratch):
    g_ref = scratch[0]
    cw = pltpu.make_async_copy(wqkv_h, wqkv, wsem.at[0])
    co = pltpu.make_async_copy(wo_h, wo, wsem.at[1])
    cw.start()
    co.start()
    for h in range(NH):
        qg[:, pl.ds(h * HD, HD)] = qg_h[...] * HD ** -0.5
        kg[:, pl.ds(h * HD, HD)] = kg_h[...]
    xyz, core = coords()
    dp, sq = lax.axis_index("dp"), lax.axis_index("seq")
    entry_barrier(partners(xyz, core))
    tok_in = Inward(tok_h, tok, 0, isend, irecv, ilocal, sq, dp)
    cot_in = Inward(cot_h, cot, 1, isend, irecv, ilocal, sq, dp)
    block_out = Outward(out, out_h, 0, osend, orecv, olocal, sq, dp)
    gtok_out = Outward(tok, gtok_h, 1, osend, orecv, olocal, sq, dp)
    for x in (tok_in, cot_in):
        for g in range(2):
            x.start(g)
    parts = [Reduce(p, xyz, core, *scratch) for p in range(PARTS)]
    cw.wait()
    co.wait()

    def forward(g, c):
        tok_in.arrive(g)
        ln_forward(g, tok, shift, scale, xh, rstd, hid)
        r = group_rows(g)
        for b in range(3):
            cs = pl.ds(b * D, D)
            proj[r, cs] = dot_nn(hid[r, :], wqkv[:, cs]).astype(BF16)
        norm_forward(g, proj, qg, kg, qn, kn, ones_in, ones_out)
        att_forward(g, proj, qn, kn, att, prob)
        out_projection(g, tok, att, wo, gate, out)
        block_out.start(g)
        return c

    lax.fori_loop(0, 2, forward, 0)
    permuted_t(3, att, idx, xt)
    for p in range(3):
        permuted_t(p, hid, idx, xt)

    def gradient(g, c):
        cot_in.arrive(g)
        grad_att(g, cot, gate, wo, gp, gatt)
        return c

    lax.fori_loop(0, 2, gradient, 0)

    def pair(p):
        return pltpu.make_async_remote_copy(
            src_ref=pout.at[p % 3], dst_ref=pin.at[p], send_sem=psend.at[p], recv_sem=precv.at[p],
            device_id=device(xyz, 1 - core), device_id_type=MESH)

    def weight(p, right):
        pout[p % 3] = dot_nn(xt[p, half(1 - core), :], right[...]).astype(BF16)
        pair(p).start()
        g_ref[p] = dot_nn(xt[p, half(core), :], right[...]).astype(BF16)

    def reduce(p):
        pair(p).wait_recv()

        def add(i, c):
            r = pl.ds(pl.multiple_of(i * 48, 16), 48)
            g_ref[p, r] = (g_ref[p, r].astype(F32) + pin[p, r].astype(F32)).astype(BF16)
            return c

        lax.fori_loop(0, 12, add, 0)
        parts[p].start()

    weight(3, gp)
    pair(3).wait_send()
    reduce(3)

    def backward(g, c):
        att_backward(g, proj, qn, kn, att, gatt, prob, ones_in)
        norm_backward(g, proj, qg, kg, qn, kn, ones_in, ones_out)
        return c

    lax.fori_loop(0, 2, backward, 0)
    parts[3].forward()
    weight(2, proj.at[:, pl.ds(2 * D, D)])
    weight(1, proj.at[:, pl.ds(D, D)])
    reduce(2)
    weight(0, proj.at[:, pl.ds(0, D)])
    reduce(1)
    parts[3].second(pad2)
    reduce(0)

    def leave(g):
        r = group_rows(g)
        gatt[r, :] = dot_nt(proj[r, :], wqkv[...]).astype(BF16)
        ln_backward(g, gatt, cot, scale, xh, rstd, tok)
        gtok_out.start(g)

    leave(0)
    parts[2].forward()
    parts[1].forward()
    leave(1)
    parts[0].forward()
    parts[3].third(pad3)
    for p in (2, 1, 0):
        parts[p].second(pad2)
    outo[...] = parts[3].finish()
    for p in (2, 1, 0):
        parts[p].third(pad3)
    for p in (2, 1, 0):
        outq[:, p * D:(p + 1) * D] = parts[p].finish()
    for p in range(3):
        pair(p).wait_send()
    for x in (tok_in, cot_in):
        for g in range(2):
            x.leave(g)
    for x in (block_out, gtok_out):
        for g in range(2):
            x.arrive(g)
            x.leave(g)


def ones_matrices():
    a = np.zeros((D, 128), np.float32)
    b = np.zeros((256, D), np.float32)
    for h in range(NH):
        a[h * HD:(h + 1) * HD, h] = 1.0
        b[h, h * HD:(h + 1) * HD] = 1.0
        b[128 + h, h * HD:(h + 1) * HD] = 1.0
    return jnp.asarray(a, BF16), jnp.asarray(b, BF16)


def on_device(tokens, mod_shift, mod_scale, res_gate, qkv_weight, out_weight, query_gain, key_gain, cotangent):
    vm = pl.BlockSpec(memory_space=pltpu.VMEM)
    anywhere = pl.BlockSpec(memory_space=pl.ANY)
    ones_in, ones_out = ones_matrices()
    pad2 = jnp.asarray(spread(36, 48), BF16)
    pad3 = jnp.asarray(np.pad(spread(9, 16), ((0, 0), (0, 12))), BF16)
    dma = pltpu.SemaphoreType.DMA
    return pl.pallas_call(
        kernel,
        out_shape=(
            jax.ShapeDtypeStruct(tokens.shape, BF16),
            jax.ShapeDtypeStruct(tokens.shape, BF16),
            jax.ShapeDtypeStruct((9, 3 * D), BF16),
            jax.ShapeDtypeStruct((9, D), BF16),
        ),
        in_specs=[anywhere] * 4 + [vm] * 10,
        out_specs=(anywhere, anywhere, vm, vm),
        scratch_shapes=[
            pltpu.VMEM((2, 16, 16, D), BF16),
            pltpu.VMEM((2, 16, 16, D), BF16),
            pltpu.VMEM((D, 3 * D), BF16),
            pltpu.VMEM((D, D), BF16),
            pltpu.VMEM((N, D), BF16),
            pltpu.VMEM((N, D), F32),
            pltpu.VMEM((N, 128), F32),
            pltpu.VMEM((N, 3 * D), BF16),
            pltpu.VMEM((N, D), BF16),
            pltpu.VMEM((N, D), BF16),
            pltpu.VMEM((N, D), BF16),
            pltpu.VMEM((2, NH, GR, GR), BF16),
            pltpu.VMEM((N, D), BF16),
            pltpu.VMEM((N, D), BF16),
            pltpu.VMEM((PARTS, D, N), BF16),
            pltpu.VMEM((2, 16, 16, D), BF16),
            pltpu.VMEM((3, 576, D), BF16),
            pltpu.VMEM((PARTS, 576, D), BF16),
            dma((2,)),
            pltpu.VMEM((1, D), F32), pltpu.VMEM((1, D), F32),
            dma((2, 2, 8)), dma((2, 2, 8)), dma((2, 2)),
            dma((2, 2, 8)), dma((2, 2, 8)), dma((2, 2)),
            dma((PARTS,)), dma((PARTS,)),
        ] + reduce_scratch(),
        compiler_params=pltpu.CompilerParams(collective_id=0, has_side_effects=True,
                                             vmem_limit_bytes=63 * 1024 * 1024),
        cost_estimate=pl.CostEstimate(flops=18 * 10**9, bytes_accessed=16 * 2**20, transcendentals=2**21),
    )(tokens, cotangent, qkv_weight, out_weight, mod_shift, mod_scale, res_gate, query_gain[None], key_gain[None],
      jnp.asarray(natural_rows()), ones_in, ones_out, pad2, pad3)


def solution(mesh):
    tok = P("dp", "seq", None, None)
    vec = P("dp", None)
    return jax.shard_map(
        on_device,
        mesh=mesh,
        in_specs=(tok, vec, vec, vec, P(), P(), P(), P(), tok),
        out_specs=(tok, tok, P(("dp", "seq"), None), P(("dp", "seq"), None)),
        check_vma=False,
    )
```
